256 devices in a mesh: grp: 2 (over z_hi), fsdp: 16 (over y, x), dp: 8 (over z_lo, core).
Axes of the slice: x: 4, y: 4, z: 8 (z_hi: 2, z_lo: 4; z = z_hi * 4 + z_lo), core: 2. Of those that a mesh axis runs over, the one named last changes fastest.
Arguments:
- acts: bfloat16 [2, 2432, 2048], P('grp', None, 'dp'), may hold values from -12 to 12
- modulation: float32 [2, 3, 2432], P('grp'), may hold values from -3 to 3
- w_in: bfloat16 [2, 9728, 2432], P('grp', 'fsdp'), may hold values from -0.125 to 0.125
- w_out: bfloat16 [2, 9728, 2432], P('grp', 'fsdp'), may hold values from -0.0625 to 0.0625
- zero_weight: bfloat16 [2432, 2432], P('fsdp'), may hold values from -0.125 to 0.125
- cotangent: bfloat16 [2, 2432, 2048], P('grp', 'fsdp', 'dp'), may hold values from -0.75 to 0.75
Outputs:
- block_out: bfloat16 [2, 2432, 2048], P('grp', 'fsdp', 'dp')
- input_grad: float32 [2, 2432, 2048], P('grp', 'fsdp', 'dp')
- zero_grad: float32 [2432, 2432], P('fsdp')
The draws below stay inside these ranges and needn't reach their ends.
All inputs are finite; a program needn't handle non-finite values.
Results may differ from the reference program's by a relative error of at most 0.0048.
Values may be sent and summed in bfloat16 or wider, within the bound.
A program may use at most 64 MiB of HBM per device.

```python
import math
from functools import partial
import jax
import jax.numpy as jnp
from jax import lax

D = 2432
HID = 9728
SEQ = 2048


def draw_acts(key, part):
    key = jax.random.fold_in(key, 17)
    noise_key, feature_key, token_key = jax.random.split(key, 3)
    feature_scale = jnp.exp(jax.random.uniform(feature_key, (2, D, 1), jnp.float32, math.log(0.3), math.log(3.0)))
    token_scale = jnp.exp(jax.random.uniform(token_key, (2, 1, SEQ), jnp.float32, math.log(0.3), math.log(3.0)))
    noise = jax.random.normal(noise_key, (2, D, SEQ), jnp.float32)
    return jnp.clip(noise * feature_scale * token_scale, -12.0, 12.0).astype(jnp.bfloat16)


def block_scale(key, extent, pieces, least, largest):
    level, own = 1.0, jax.random.fold_in(key, 6)
    for dim, blocks in pieces:
        draws = jnp.exp(jax.random.uniform(jax.random.fold_in(own, dim), (blocks,), jnp.float32, least / len(pieces), largest / len(pieces)))
        level = level * jnp.repeat(draws, extent[dim] // blocks).reshape([-1 if axis == dim else 1 for axis in range(len(extent))])
    return level


def normal_values(rng, shape, scale, bound, pieces=(), dtype=jnp.bfloat16):
    entries = scale * jax.random.normal(rng, shape, jnp.float32)
    if pieces:
        entries = entries * block_scale(rng, shape, pieces, -0.22, 0.18)
    return jnp.clip(entries, -bound, bound).astype(dtype)


def setup_inputs(seed: int = 0) -> dict:
    arg_keys = jax.random.split(jax.random.key(seed), 7)
    return {
        "acts": draw_acts(jax.random.fold_in(arg_keys[6], 71), 0),
        "modulation": normal_values(arg_keys[1], (2, 3, D), 1.0, 3.0, ((0, 2),), jnp.float32),
        "w_in": normal_values(arg_keys[2], (2, HID, D), D ** -0.5, 0.125, ((0, 2), (1, 16))),
        "w_out": normal_values(arg_keys[3], (2, HID, D), HID ** -0.5, 0.0625, ((0, 2), (1, 16))),
        "zero_weight": normal_values(arg_keys[4], (D, D), D ** -0.5, 0.125, ((0, 16),)),
        "cotangent": normal_values(arg_keys[5], (2, D, SEQ), 0.125, 0.75, ((0, 2), (1, 16), (2, 8))),
    }


EPSILON = 1e-06

def layer_norm(values, mod_shift, mod_scale):
    token_mean = lax.optimization_barrier(jnp.mean(values, axis=0, keepdims=True))
    centred = values - token_mean
    variance = lax.optimization_barrier(jnp.mean(centred * centred, axis=0, keepdims=True))
    return centred * lax.rsqrt(variance + EPSILON) * (1.0 + mod_scale[:, None]) + mod_shift[:, None]

def gelu_tanh(values):
    return jax.nn.gelu(values, approximate=True)

def contract_rows(weights, columns):
    return lax.dot_general(weights, columns, (((0,), (0,)), ((), ())), preferred_element_type=jnp.float32)

def reference(acts, modulation, w_in, w_out, zero_weight, cotangent):
    saved = []
    sums = []
    for group in range(2):
        values = acts[group].astype(jnp.float32)
        normed = layer_norm(values, modulation[group, 0], modulation[group, 1]).astype(jnp.bfloat16)
        pre_act = jnp.dot(w_in[group], normed, preferred_element_type=jnp.float32)
        hidden = gelu_tanh(pre_act).astype(jnp.bfloat16)
        branch = contract_rows(w_out[group], hidden)
        saved.append((values, pre_act))
        sums.append(values + modulation[group, 2][:, None] * branch)
    control_out = sums[0].astype(jnp.bfloat16)
    residual = jnp.dot(zero_weight, control_out, preferred_element_type=jnp.float32)
    base_out = (sums[1] + residual).astype(jnp.bfloat16)
    zero_grad = lax.dot_general(cotangent[1], control_out, (((1,), (1,)), ((), ())), preferred_element_type=jnp.float32)
    control_up = contract_rows(zero_weight, cotangent[1]) + cotangent[0].astype(jnp.float32)
    upstreams = (control_up, cotangent[1].astype(jnp.float32))
    grads = []
    for group in range(2):
        values, pre_act = saved[group]
        gate_grad = (modulation[group, 2][:, None] * upstreams[group]).astype(jnp.bfloat16)
        hidden_grad = jnp.dot(w_out[group], gate_grad, preferred_element_type=jnp.float32)
        pre_grad = jax.vjp(gelu_tanh, pre_act)[1](hidden_grad)[0].astype(jnp.bfloat16)
        norm_grad = contract_rows(w_in[group], pre_grad)
        norm_map = partial(layer_norm, mod_shift=modulation[group, 0], mod_scale=modulation[group, 1])
        norm_back = jax.vjp(norm_map, values)[1]
        grads.append(upstreams[group] + norm_back(norm_grad)[0])
    return (jnp.stack([control_out, base_out]), jnp.stack(grads), zero_grad)
```

```python
from functools import partial

import jax
import jax.numpy as jnp
from jax import lax
from jax.experimental import pallas as pl
from jax.experimental.pallas import tpu as pltpu
from jax.sharding import PartitionSpec as P

MESH = pl.DeviceIdType.MESH
F32 = jnp.float32
BF16 = jnp.bfloat16
EPSILON = 1e-06
D = 2432
B = 152
H = 608
N = 256
L = 128
OWN = 192
GELU_C = 0.7978845608028654
TILES = ((0, 640), (640, 640), (1280, 640), (1920, 512))

C1, C2, B1, B2, G1, G2, O1, O2, N1, N2 = range(10)


def contract_rows(a, b):
    return lax.dot_general(a, b, (((0,), (0,)), ((), ())), preferred_element_type=F32)


def kernel(
    acts_h, mod_h, win_h, wout_h, zw_h, cot_h,
    block_o, grad_o, zero_o,
    acts, mod, win, wout, zw, cot, in_sem,
    cols, xf, normed, pre, dgelu, hidden, T, stat,
    sC, rC1, mC32, mC16, rC2,
    sB, rB1, mB32, mB16, rB2,
    sN, rN1, mN32, mN16, rN2,
    GG, GO, a2d, rows32, up32,
    carr_s, carr_r, co_s, co_r,
    st_s1, st_r1, st_s2, st_r2,
    zf, F16, zr1, H32, H16, zr2, A16, A16b,
    ss, rs, st_ss, st_rs, g_ss, g_rs, c_ss, c_rs, z2_ss, z2_rs, z3_ss, z3_rs,
):
    g = lax.axis_index("grp")
    f = lax.axis_index("fsdp")
    d = lax.axis_index("dp")
    y, x = f // 4, f % 4
    z, c = d // 2, d % 2
    pos = g * 4 + z
    control = g == 0
    base = g == 1

    def at_xy(py, px):
        return (g, py * 4 + px, d)

    def at_z(q):
        return (q // 4, f, (q % 4) * 2 + c)

    sibling = (g, f, z * 2 + (1 - c))
    partner = (1 - g, f, d)

    loads = []
    for i, (src, dst) in enumerate(
        ((cot_h.at[0], cot), (zw_h, zw), (mod_h.at[0], mod), (acts_h.at[0], acts), (win_h.at[0], win), (wout_h.at[0], wout))
    ):
        cp = pltpu.make_async_copy(src, dst, in_sem.at[i])
        cp.start()
        loads.append(cp)
    l_cot, l_zw, l_mod, l_acts, l_win, l_wout = loads

    barrier = pltpu.get_barrier_semaphore()
    for k in (1, 2, 3):
        pl.semaphore_signal(barrier, inc=1, device_id=at_xy(y, (x + k) % 4), device_id_type=MESH)
        pl.semaphore_signal(barrier, inc=1, device_id=at_xy((y + k) % 4, x), device_id_type=MESH)
    for k in range(1, 8):
        pl.semaphore_signal(barrier, inc=1, device_id=at_z((pos + k) % 8), device_id_type=MESH)
    pl.semaphore_signal(barrier, inc=1, device_id=sibling, device_id_type=MESH)

    def remote(src, dst, send, recv, where):
        return pltpu.make_async_remote_copy(
            src_ref=src, dst_ref=dst, send_sem=send, recv_sem=recv, device_id=where, device_id_type=MESH
        )

    HK = [(h, k) for k in (1, 3, 2) for h in (0, 1)]

    def peer_x(k):
        return at_xy(y, (x + k) % 4)

    def peer_y(k):
        return at_xy((y + k) % 4, x)

    def rs1(n, s, r1):
        out = []
        for h, k in HK:
            to = (x + k) % 4 if h == 0 else (y + k) % 4
            where = peer_x(k) if h == 0 else peer_y(k)
            out.append(remote(s.at[h, to], r1.at[h, k - 1], ss.at[n, h, k - 1], rs.at[n, h, k - 1], where))
        return out

    def rs2(n, m16, r2):
        out = []
        for h, k in HK:
            to = (y + k) % 4 if h == 0 else (x + k) % 4
            where = peer_y(k) if h == 0 else peer_x(k)
            out.append(remote(m16.at[h, to], r2.at[h, k - 1], ss.at[n, h, k - 1], rs.at[n, h, k - 1], where))
        return out

    def ag1(n, G):
        out = []
        for h, k in HK:
            blk = G.at[0, x, y] if h == 0 else G.at[1, y, x]
            where = peer_y(k) if h == 0 else peer_x(k)
            out.append(remote(blk, blk, ss.at[n, h, k - 1], rs.at[n, h, k - 1], where))
        return out

    def ag2(n, G):
        out = []
        for h, k in HK:
            blk = G.at[0, x] if h == 0 else G.at[1, y]
            where = peer_x(k) if h == 0 else peer_y(k)
            out.append(remote(blk, blk, ss.at[n, h, k - 1], rs.at[n, h, k - 1], where))
        return out

    def start(copies):
        for cp in copies:
            cp.start()

    def arrived(copies):
        for cp in copies:
            cp.wait_recv()

    def sent(copies):
        for cp in copies:
            cp.wait_send()

    def extract(s):
        def body(i, _):
            blk = T[pl.ds(pl.multiple_of(i * B, 8), B), :]
            s[0, i % 4, i // 4] = blk[:, :L].astype(BF16)
            s[1, i // 4, i % 4] = blk[:, L:].astype(BF16)
            return 0

        lax.fori_loop(0, 16, body, 0)

    def rs_mid(s, r1, m32, m16):
        def body(q, _):
            for h in (0, 1):
                own = x if h == 0 else y
                total = s[h, own, q].astype(F32)
                for k in range(3):
                    total = total + r1[h, k, q].astype(F32)
                m32[h, q] = total
                m16[h, q] = total.astype(BF16)
            return 0

        lax.fori_loop(0, 4, body, 0)

    def rs_last(m32, r2, out):
        for h in (0, 1):
            total = m32[h, y if h == 0 else x]
            for k in range(3):
                total = total + r2[h, k].astype(F32)
            out[:, h * L : (h + 1) * L] = total

    def flatten(G):
        def body(i, _):
            yy, xx = i // 2, 2 * (i % 2)
            rows = pl.ds(pl.multiple_of(i * 2 * B, 16), 2 * B)
            for h in (0, 1):
                p, q = (G[0, xx, yy], G[0, xx + 1, yy]) if h == 0 else (G[1, yy, xx], G[1, yy, xx + 1])
                both = jnp.concatenate([p.astype(F32), q.astype(F32)], axis=0)
                a2d[rows, h * L : (h + 1) * L] = both.astype(BF16)
            return 0

        lax.fori_loop(0, 8, body, 0)

    copies_c1, copies_c2 = rs1(C1, sC, rC1), rs2(C2, mC16, rC2)
    copies_b1, copies_b2 = rs1(B1, sB, rB1), rs2(B2, mB16, rB2)
    copies_n1, copies_n2 = rs1(N1, sN, rN1), rs2(N2, mN16, rN2)
    copies_g1, copies_g2 = ag1(G1, GG), ag2(G2, GG)
    copies_o1, copies_o2 = ag1(O1, GO), ag2(O2, GO)
    carr_copy = remote(carr_s, carr_r, g_ss.at[0], g_rs.at[0], partner)
    co_copy = remote(co_s, co_r, g_ss.at[1], g_rs.at[1], partner)
    st1 = [remote(st_s1, st_r1.at[k - 1], st_ss.at[0, k - 1], st_rs.at[0, k - 1], peer_x(k)) for k in (1, 2, 3)]
    st2 = [remote(st_s2, st_r2.at[k - 1], st_ss.at[1, k - 1], st_rs.at[1, k - 1], peer_y(k)) for k in (1, 2, 3)]
    z1 = remote(F16.at[1 - c], zr1, c_ss.at[0], c_rs.at[0], sibling)
    z2 = [
        remote(H16.at[(pos + k) % 8], zr2.at[z], z2_ss.at[k - 1], z2_rs.at[z], at_z((pos + k) % 8))
        for k in (1, 7, 2, 6, 3, 5, 4)
    ]
    z3 = [
        remote(A16.at[pos], A16.at[pos], z3_ss.at[k - 1], z3_rs.at[k - 1], at_z((pos + k) % 8))
        for k in (1, 7, 2, 6, 3, 5, 4)
    ]
    z4 = remote(A16, A16b, c_ss.at[1], c_rs.at[1], sibling)

    def z2_arrival(zz):
        return remote(H16.at[0], zr2.at[zz], z2_ss.at[0], z2_rs.at[zz], sibling)

    l_cot.wait()
    l_zw.wait()

    @pl.when(base)
    def _():
        for c0, width in TILES:
            T[c0 : c0 + width, :] = contract_rows(zw[:, c0 : c0 + width], cot[...])
        extract(sC)

    pl.semaphore_wait(barrier, 14)

    @pl.when(base)
    def _():
        start(copies_c1)

    l_mod.wait()
    l_acts.wait()

    def column_body(j, _):
        at = pl.ds(pl.multiple_of(j * L, L), L)
        row = lax.broadcasted_iota(jnp.int32, (8, L), 0)
        m = mod[:, at]
        three = jnp.where(row == 0, m[0:1, :], jnp.where(row == 1, 1.0 + m[1:2, :], m[2:3, :]))
        cols[at, 0:8] = jnp.transpose(three)
        return 0

    lax.fori_loop(0, D // L, column_body, 0)

    def fold(v):
        return jnp.sum(v.reshape(L // 8, 8, N), axis=0)

    def sum_body(j, acc):
        at = pl.ds(pl.multiple_of(j * L, L), L)
        v = acts[at, :].astype(F32)
        xf[at, :] = v
        return acc + fold(v)

    zeros8 = jnp.zeros((8, N), F32)
    mean = jnp.sum(lax.fori_loop(0, D // L, sum_body, zeros8), axis=0, keepdims=True) * (1.0 / D)

    def var_body(j, acc):
        at = pl.ds(pl.multiple_of(j * L, L), L)
        v = xf[at, :] - mean
        return acc + fold(v * v)

    variance = jnp.sum(lax.fori_loop(0, D // L, var_body, zeros8), axis=0, keepdims=True) * (1.0 / D)
    rstd = lax.rsqrt(variance + EPSILON)
    stat[0:1, :] = mean
    stat[1:2, :] = rstd

    def norm_body(j, _):
        at = pl.ds(pl.multiple_of(j * L, L), L)
        v = (xf[at, :] - mean) * rstd
        normed[at, :] = (v * cols[at, 1:2] + cols[at, 0:1]).astype(BF16)
        return 0

    lax.fori_loop(0, D // L, norm_body, 0)

    l_win.wait()
    half = H // 2
    for i in range(2):
        pre[i * half : (i + 1) * half, :] = jnp.dot(
            win[i * half : (i + 1) * half, :], normed[...], preferred_element_type=F32
        )

    def gelu_body(j, _):
        at = pl.ds(pl.multiple_of(j * 32, 32), 32)
        v = pre[at, :]
        v2 = v * v
        t = jnp.tanh(GELU_C * (v + 0.044715 * (v2 * v)))
        cdf = 0.5 * (1.0 + t)
        hidden[at, :] = (v * cdf).astype(BF16)
        dgelu[at, :] = cdf + 0.5 * v * (1.0 - t * t) * (GELU_C * (1.0 + 3.0 * 0.044715 * v2))
        return 0

    lax.fori_loop(0, H // 32, gelu_body, 0)
    l_wout.wait()
    for c0, width in TILES:
        T[c0 : c0 + width, :] = contract_rows(wout[:, c0 : c0 + width], hidden[...])
    extract(sB)
    start(copies_b1)

    own_rows = pl.ds(pl.multiple_of(f * B, 8), B)
    gate_rows = cols[own_rows, 2:3]

    def set_gate_grad(up):
        gg = (gate_rows * up).astype(BF16)
        GG[0, x, y] = gg[:, :L]
        GG[1, y, x] = gg[:, L:]

    @pl.when(base)
    def _():
        arrived(copies_c1)
        rs_mid(sC, rC1, mC32, mC16)
        start(copies_c2)
        up = cot[...].astype(F32)
        up32[...] = up
        set_gate_grad(up)
        start(copies_g1)
        arrived(copies_c2)
        rs_last(mC32, rC2, rows32)
        carr_s[...] = rows32[...].astype(BF16)
        carr_copy.start()
        arrived(copies_g1)
        start(copies_g2)

    arrived(copies_b1)
    rs_mid(sB, rB1, mB32, mB16)
    start(copies_b2)
    arrived(copies_b2)
    rs_last(mB32, rB2, rows32)
    rows32[...] = xf[own_rows, :] + gate_rows * rows32[...]

    @pl.when(control)
    def _():
        out = rows32[...].astype(BF16)
        block_o[...] = out
        co_s[...] = out
        co_copy.start()
        carr_copy.wait_recv()
        up = carr_r[...].astype(F32) + cot[...].astype(F32)
        up32[...] = up
        set_gate_grad(up)
        start(copies_g1)
        arrived(copies_g1)
        start(copies_g2)

    arrived(copies_g2)
    flatten(GG)
    for i in range(2):
        hg = jnp.dot(wout[i * half : (i + 1) * half, :], a2d[...], preferred_element_type=F32)
        hidden[i * half : (i + 1) * half, :] = (hg * dgelu[i * half : (i + 1) * half, :]).astype(BF16)
    for c0, width in TILES:
        T[c0 : c0 + width, :] = contract_rows(win[:, c0 : c0 + width], hidden[...])
    extract(sN)

    def stat_body(j, acc):
        at = pl.ds(pl.multiple_of(j * L, L), L)
        v = T[at, :] * cols[at, 1:2]
        xhat = (xf[at, :] - stat[0:1, :]) * stat[1:2, :]
        return acc[0] + fold(v), acc[1] + fold(v * xhat)

    start(copies_n1)
    p1, p2 = lax.fori_loop(0, D // L, stat_body, (zeros8, zeros8))
    st_s1[0:8, :] = p1
    st_s1[8:16, :] = p2
    start(st1)

    @pl.when(base)
    def _():
        co_copy.wait_recv()
        GO[0, x, y] = co_r[:, :L]
        GO[1, y, x] = co_r[:, L:]
        start(copies_o1)
        arrived(copies_o1)
        start(copies_o2)
        arrived(copies_o2)
        flatten(GO)
        zf[19 * B :, :] = jnp.zeros((16 * OWN - 19 * B, L), F32)
        for c0, width in TILES:
            term = lax.dot_general(
                cot[...], a2d[c0 : c0 + width, :], (((1,), (1,)), ((), ())), preferred_element_type=F32
            )
            for t in range(width // L):
                r0 = (c0 // L + t) * B
                zf[r0 : r0 + B, :] = term[:, t * L : (t + 1) * L]

        def flat_body(o, _):
            F16[o // 8, o % 8] = zf[pl.ds(pl.multiple_of(o * OWN, OWN), OWN), :].astype(BF16)
            return 0

        lax.fori_loop(0, 16, flat_body, 0)
        z1.start()
        residual = jnp.dot(zw[...], a2d[...], preferred_element_type=F32)
        block_o[...] = (rows32[...] + residual).astype(BF16)
        z1.wait_recv()

        def pair_body(q, _):
            total = zf[pl.ds(pl.multiple_of((c * 8 + q) * OWN, OWN), OWN), :] + zr1[q].astype(F32)
            H32[q] = total
            H16[q] = total.astype(BF16)
            return 0

        lax.fori_loop(0, 8, pair_body, 0)
        start(z2)

    arrived(copies_n1)
    rs_mid(sN, rN1, mN32, mN16)
    start(copies_n2)
    arrived(st1)
    st_s2[...] = st_s1[...] + st_r1[0] + st_r1[1] + st_r1[2]
    start(st2)
    arrived(copies_n2)
    arrived(st2)
    rs_last(mN32, rN2, rows32)
    both = st_s2[...] + st_r2[0] + st_r2[1] + st_r2[2]
    m1 = jnp.sum(both[0:8, :], axis=0, keepdims=True) * (1.0 / D)
    m2 = jnp.sum(both[8:16, :], axis=0, keepdims=True) * (1.0 / D)
    xhat = (xf[own_rows, :] - stat[0:1, :]) * stat[1:2, :]
    ghat = rows32[...] * cols[own_rows, 1:2]
    grad_o[...] = up32[...] + stat[1:2, :] * (ghat - m1 - xhat * m2)

    @pl.when(base)
    def _():
        for k in (1, 2, 3):
            z2_arrival((z + k) % 4).wait_recv()
        total = H32[pos]
        for k in (1, 2, 3):
            total = total + zr2[(z + k) % 4].astype(F32)
        A16[pos] = total.astype(BF16)

    @pl.when(control)
    def _():
        for k in range(4):
            z2_arrival(k).wait_recv()
        total = zr2[0].astype(F32)
        for k in (1, 2, 3):
            total = total + zr2[k].astype(F32)
        A16[pos] = total.astype(BF16)

    start(z3)
    arrived(z3)
    z4.start()

    def own_body(q, _):
        zf[pl.ds(pl.multiple_of((c * 8 + q) * OWN, OWN), OWN), :] = A16[q].astype(F32)
        return 0

    lax.fori_loop(0, 8, own_body, 0)
    z4.wait_recv()

    def other_body(q, _):
        zf[pl.ds(pl.multiple_of(((1 - c) * 8 + q) * OWN, OWN), OWN), :] = A16b[q].astype(F32)
        return 0

    lax.fori_loop(0, 8, other_body, 0)
    for t in range(19):
        zero_o[:, t * L : (t + 1) * L] = zf[t * B : (t + 1) * B, :].astype(BF16)

    sent(copies_b1 + copies_b2 + copies_g1 + copies_g2 + copies_n1 + copies_n2 + st1 + st2 + z3 + [z4])

    @pl.when(base)
    def _():
        sent(copies_c1 + copies_c2 + copies_o1 + copies_o2 + z2 + [carr_copy, z1])

    @pl.when(control)
    def _():
        co_copy.wait_send()


def local(acts, modulation, w_in, w_out, zero_weight, cotangent):
    vm = pltpu.VMEM
    dma = pltpu.SemaphoreType.DMA

    def rs_bufs():
        return [vm((2, 4, 4, B, L), BF16), vm((2, 3, 4, B, L), BF16), vm((2, 4, B, L), F32), vm((2, 4, B, L), BF16), vm((2, 3, B, L), BF16)]

    scratch = [
        vm((D, N), BF16), vm((3, D), F32), vm((H, D), BF16), vm((H, D), BF16), vm((B, D), BF16), vm((B, N), BF16), dma((6,)),
        vm((D, L), F32), vm((D, N), F32), vm((D, N), BF16), vm((H, N), F32), vm((H, N), F32), vm((H, N), BF16), vm((D, N), F32), vm((8, N), F32),
        *rs_bufs(), *rs_bufs(), *rs_bufs(),
        vm((2, 4, 4, B, L), BF16), vm((2, 4, 4, B, L), BF16), vm((D, N), BF16), vm((B, N), F32), vm((B, N), F32),
        vm((B, N), BF16), vm((B, N), BF16), vm((B, N), BF16), vm((B, N), BF16),
        vm((16, N), F32), vm((3, 16, N), F32), vm((16, N), F32), vm((3, 16, N), F32),
        vm((16 * OWN, L), F32), vm((2, 8, OWN, L), BF16), vm((8, OWN, L), BF16), vm((8, OWN, L), F32), vm((8, OWN, L), BF16),
        vm((4, OWN, L), BF16), vm((8, OWN, L), BF16), vm((8, OWN, L), BF16),
        dma((10, 2, 3)), dma((10, 2, 3)), dma((2, 3)), dma((2, 3)), dma((2,)), dma((2,)), dma((2,)), dma((2,)),
        dma((7,)), dma((4,)), dma((7,)), dma((7,)),
    ]
    block, grad, zero = pl.pallas_call(
        kernel,
        out_shape=(
            jax.ShapeDtypeStruct((B, N), BF16),
            jax.ShapeDtypeStruct((B, N), F32),
            jax.ShapeDtypeStruct((B, D), BF16),
        ),
        in_specs=[pl.BlockSpec(memory_space=pl.ANY)] * 6,
        out_specs=[pl.BlockSpec(memory_space=pltpu.VMEM)] * 3,
        scratch_shapes=scratch,
        compiler_params=pltpu.CompilerParams(
            collective_id=0, has_side_effects=True, vmem_limit_bytes=60 * 2**20
        ),
    )(acts, modulation, w_in, w_out, zero_weight, cotangent)
    return block[None], grad[None], zero.astype(F32)


def solution(mesh):
    placed = (
        P("grp", None, "dp"),
        P("grp", None, None),
        P("grp", "fsdp", None),
        P("grp", "fsdp", None),
        P("fsdp", None),
        P("grp", "fsdp", "dp"),
    )
    return jax.shard_map(
        local,
        mesh=mesh,
        in_specs=placed,
        out_specs=(P("grp", "fsdp", "dp"), P("grp", "fsdp", "dp"), P("fsdp", None)),
        check_vma=False,
    )
```

```python
from functools import partial

import jax
import jax.numpy as jnp
from jax import lax
from jax.experimental import pallas as pl
from jax.experimental.pallas import tpu as pltpu
from jax.sharding import PartitionSpec as P

MESH = pl.DeviceIdType.MESH
F32 = jnp.float32
BF16 = jnp.bfloat16
EPSILON = 1e-06
D = 2432
B = 152
H = 608
N = 256
L = 128
OWN = 192
GELU_C = 0.7978845608028654
TILES = ((0, 640), (640, 640), (1280, 640), (1920, 512))

C1, C2, B1, B2, G1, G2, O1, O2, N1, N2 = range(10)


def contract_rows(a, b):
    return lax.dot_general(a, b, (((0,), (0,)), ((), ())), preferred_element_type=F32)


def kernel(
    acts_h, mod_h, win_h, wout_h, zw_h, cot_h,
    block_o, grad_o, A16,
    acts, mod, win, wout, zw, cot, in_sem,
    cols, xf, normed, pre, dgelu, hidden, T, stat,
    sC, rC1, mC32, mC16, rC2,
    sB, rB1, mB32, mB16, rB2,
    sN, rN1, mN32, mN16, rN2,
    GG, GO, a2d, rows32, up32,
    carr_s, carr_r, co_s, co_r,
    st_s1, st_r1, st_s2, st_r2,
    cot1_r, zf, F16, zr1, H32, H16, zr2,
    ss, rs, st_ss, st_rs, g_ss, g_rs, c_ss, c_rs, z2_ss, z2_rs, z3_ss, z3_rs,
):
    g = lax.axis_index("grp")
    f = lax.axis_index("fsdp")
    d = lax.axis_index("dp")
    y, x = f // 4, f % 4
    z, c = d // 2, d % 2
    pos = g * 4 + z
    control = g == 0
    base = g == 1

    def at_xy(py, px):
        return (g, py * 4 + px, d)

    def at_z(q):
        return (q // 4, f, (q % 4) * 2 + c)

    sibling = (g, f, z * 2 + (1 - c))
    partner = (1 - g, f, d)

    loads = []
    for i, (src, dst) in enumerate(
        ((cot_h.at[0], cot), (zw_h, zw), (mod_h, mod), (acts_h.at[0], acts), (win_h.at[0], win), (wout_h.at[0], wout))
    ):
        cp = pltpu.make_async_copy(src, dst, in_sem.at[i])
        cp.start()
        loads.append(cp)
    l_cot, l_zw, l_mod, l_acts, l_win, l_wout = loads

    barrier = pltpu.get_barrier_semaphore()
    for k in (1, 2, 3):
        pl.semaphore_signal(barrier, inc=1, device_id=at_xy(y, (x + k) % 4), device_id_type=MESH)
        pl.semaphore_signal(barrier, inc=1, device_id=at_xy((y + k) % 4, x), device_id_type=MESH)
    for k in range(1, 8):
        pl.semaphore_signal(barrier, inc=1, device_id=at_z((pos + k) % 8), device_id_type=MESH)
    pl.semaphore_signal(barrier, inc=1, device_id=sibling, device_id_type=MESH)

    def remote(src, dst, send, recv, where):
        return pltpu.make_async_remote_copy(
            src_ref=src, dst_ref=dst, send_sem=send, recv_sem=recv, device_id=where, device_id_type=MESH
        )

    HK = [(h, k) for k in (1, 3, 2) for h in (0, 1)]

    def peer_x(k):
        return at_xy(y, (x + k) % 4)

    def peer_y(k):
        return at_xy((y + k) % 4, x)

    def rs1(n, s, r1):
        out = []
        for h, k in HK:
            to = (x + k) % 4 if h == 0 else (y + k) % 4
            where = peer_x(k) if h == 0 else peer_y(k)
            out.append(remote(s.at[h, to], r1.at[h, k - 1], ss.at[n, h, k - 1], rs.at[n, h, k - 1], where))
        return out

    def rs2(n, m16, r2):
        out = []
        for h, k in HK:
            to = (y + k) % 4 if h == 0 else (x + k) % 4
            where = peer_y(k) if h == 0 else peer_x(k)
            out.append(remote(m16.at[h, to], r2.at[h, k - 1], ss.at[n, h, k - 1], rs.at[n, h, k - 1], where))
        return out

    def ag1(n, G):
        out = []
        for h, k in HK:
            blk = G.at[0, x, y] if h == 0 else G.at[1, y, x]
            where = peer_y(k) if h == 0 else peer_x(k)
            out.append(remote(blk, blk, ss.at[n, h, k - 1], rs.at[n, h, k - 1], where))
        return out

    def ag2(n, G):
        out = []
        for h, k in HK:
            blk = G.at[0, x] if h == 0 else G.at[1, y]
            where = peer_x(k) if h == 0 else peer_y(k)
            out.append(remote(blk, blk, ss.at[n, h, k - 1], rs.at[n, h, k - 1], where))
        return out

    def start(copies):
        for cp in copies:
            cp.start()

    def arrived(copies):
        for cp in copies:
            cp.wait_recv()

    def sent(copies):
        for cp in copies:
            cp.wait_send()

    def extract(s):
        def body(i, _):
            blk = T[pl.ds(pl.multiple_of(i * B, 8), B), :]
            s[0, i % 4, i // 4] = blk[:, :L].astype(BF16)
            s[1, i // 4, i % 4] = blk[:, L:].astype(BF16)
            return 0

        lax.fori_loop(0, 16, body, 0)

    def rs_mid(s, r1, m32, m16):
        def body(q, _):
            for h in (0, 1):
                own = x if h == 0 else y
                total = s[h, own, q].astype(F32)
                for k in range(3):
                    total = total + r1[h, k, q].astype(F32)
                m32[h, q] = total
                m16[h, q] = total.astype(BF16)
            return 0

        lax.fori_loop(0, 4, body, 0)

    def rs_last(m32, r2, out):
        for h in (0, 1):
            total = m32[h, y if h == 0 else x]
            for k in range(3):
                total = total + r2[h, k].astype(F32)
            out[:, h * L : (h + 1) * L] = total

    def flatten(G):
        def body(i, _):
            yy, xx = i // 2, 2 * (i % 2)
            rows = pl.ds(pl.multiple_of(i * 2 * B, 16), 2 * B)
            for h in (0, 1):
                p, q = (G[0, xx, yy], G[0, xx + 1, yy]) if h == 0 else (G[1, yy, xx], G[1, yy, xx + 1])
                both = jnp.concatenate([p.astype(F32), q.astype(F32)], axis=0)
                a2d[rows, h * L : (h + 1) * L] = both.astype(BF16)
            return 0

        lax.fori_loop(0, 8, body, 0)

    copies_c1, copies_c2 = rs1(C1, sC, rC1), rs2(C2, mC16, rC2)
    copies_b1, copies_b2 = rs1(B1, sB, rB1), rs2(B2, mB16, rB2)
    copies_n1, copies_n2 = rs1(N1, sN, rN1), rs2(N2, mN16, rN2)
    copies_g1, copies_g2 = ag1(G1, GG), ag2(G2, GG)
    copies_o1, copies_o2 = ag1(O1, GO), ag2(O2, GO)
    carr_copy = remote(carr_s, carr_r, g_ss.at[0], g_rs.at[0], partner)
    co_copy = remote(co_s, co_r, g_ss.at[1], g_rs.at[1], partner)
    cot_copy = remote(cot, cot1_r, g_ss.at[2], g_rs.at[2], partner)
    st1 = [remote(st_s1, st_r1.at[k - 1], st_ss.at[0, k - 1], st_rs.at[0, k - 1], peer_x(k)) for k in (1, 2, 3)]
    st2 = [remote(st_s2, st_r2.at[k - 1], st_ss.at[1, k - 1], st_rs.at[1, k - 1], peer_y(k)) for k in (1, 2, 3)]
    z1 = remote(F16.at[1 - c], zr1, c_ss.at[0], c_rs.at[0], sibling)
    z2 = [
        remote(H16.at[(pos + k) % 8], zr2.at[z], z2_ss.at[k - 1], z2_rs.at[z], at_z((pos + k) % 8))
        for k in (1, 7, 2, 6, 3, 5, 4)
    ]
    z3 = [
        remote(A16.at[c, pos], A16.at[c, pos], z3_ss.at[k - 1], z3_rs.at[k - 1], at_z((pos + k) % 8))
        for k in (1, 7, 2, 6, 3, 5, 4)
    ]
    z4 = remote(A16.at[c], A16.at[c], c_ss.at[1], c_rs.at[1], sibling)

    def z2_arrival(zz):
        return remote(H16.at[0], zr2.at[zz], z2_ss.at[0], z2_rs.at[zz], sibling)

    l_cot.wait()
    l_zw.wait()

    @pl.when(base)
    def _():
        for c0, width in TILES:
            T[c0 : c0 + width, :] = contract_rows(zw[:, c0 : c0 + width], cot[...])
        extract(sC)

    pl.semaphore_wait(barrier, 14)

    @pl.when(base)
    def _():
        start(copies_c1)
        cot_copy.start()

    l_mod.wait()
    l_acts.wait()

    def column_body(j, _):
        at = pl.ds(pl.multiple_of(j * L, L), L)
        row = lax.broadcasted_iota(jnp.int32, (8, L), 0)
        three = jnp.where(row == 0, mod[0, :, at], jnp.where(row == 1, 1.0 + mod[1, :, at], mod[2, :, at]))
        cols[at, 0:8] = jnp.transpose(three)
        return 0

    lax.fori_loop(0, D // L, column_body, 0)

    def fold(v):
        return jnp.sum(v.reshape(L // 8, 8, N), axis=0)

    def sum_body(j, acc):
        at = pl.ds(pl.multiple_of(j * L, L), L)
        v = acts[at, :].astype(F32)
        xf[at, :] = v
        return acc + fold(v)

    zeros8 = jnp.zeros((8, N), F32)
    mean = jnp.sum(lax.fori_loop(0, D // L, sum_body, zeros8), axis=0, keepdims=True) * (1.0 / D)

    def var_body(j, acc):
        at = pl.ds(pl.multiple_of(j * L, L), L)
        v = xf[at, :] - mean
        return acc + fold(v * v)

    variance = jnp.sum(lax.fori_loop(0, D // L, var_body, zeros8), axis=0, keepdims=True) * (1.0 / D)
    rstd = lax.rsqrt(variance + EPSILON)
    stat[0:1, :] = mean
    stat[1:2, :] = rstd

    def norm_body(j, _):
        at = pl.ds(pl.multiple_of(j * L, L), L)
        v = (xf[at, :] - mean) * rstd
        normed[at, :] = (v * cols[at, 1:2] + cols[at, 0:1]).astype(BF16)
        return 0

    lax.fori_loop(0, D // L, norm_body, 0)

    l_win.wait()
    half = H // 2
    for i in range(2):
        pre[i * half : (i + 1) * half, :] = jnp.dot(
            win[i * half : (i + 1) * half, :], normed[...], preferred_element_type=F32
        )

    def gelu_body(j, _):
        at = pl.ds(pl.multiple_of(j * 32, 32), 32)
        v = pre[at, :]
        v2 = v * v
        t = jnp.tanh(GELU_C * (v + 0.044715 * (v2 * v)))
        cdf = 0.5 * (1.0 + t)
        hidden[at, :] = (v * cdf).astype(BF16)
        dgelu[at, :] = cdf + 0.5 * v * (1.0 - t * t) * (GELU_C * (1.0 + 3.0 * 0.044715 * v2))
        return 0

    lax.fori_loop(0, H // 32, gelu_body, 0)
    l_wout.wait()
    for c0, width in TILES:
        T[c0 : c0 + width, :] = contract_rows(wout[:, c0 : c0 + width], hidden[...])
    extract(sB)

    @pl.when(control)
    def _():
        start(copies_b1)

    own_rows = pl.ds(pl.multiple_of(f * B, 8), B)
    gate_rows = cols[own_rows, 2:3]

    def set_gate_grad(up):
        gg = (gate_rows * up).astype(BF16)
        GG[0, x, y] = gg[:, :L]
        GG[1, y, x] = gg[:, L:]

    @pl.when(base)
    def _():
        arrived(copies_c1)
        rs_mid(sC, rC1, mC32, mC16)
        start(copies_c2)
        up = cot[...].astype(F32)
        up32[...] = up
        set_gate_grad(up)
        start(copies_g1)
        arrived(copies_c2)
        rs_last(mC32, rC2, rows32)
        carr_s[...] = rows32[...].astype(BF16)
        carr_copy.start()
        start(copies_b1)
        arrived(copies_g1)
        start(copies_g2)

    arrived(copies_b1)
    rs_mid(sB, rB1, mB32, mB16)
    start(copies_b2)
    arrived(copies_b2)
    rs_last(mB32, rB2, rows32)
    rows32[...] = xf[own_rows, :] + gate_rows * rows32[...]

    @pl.when(control)
    def _():
        out = rows32[...].astype(BF16)
        block_o[...] = out
        co_s[...] = out
        co_copy.start()
        GO[0, x, y] = out[:, :L]
        GO[1, y, x] = out[:, L:]
        start(copies_o1)
        carr_copy.wait_recv()
        up = carr_r[...].astype(F32) + cot[...].astype(F32)
        up32[...] = up
        set_gate_grad(up)
        start(copies_g1)
        arrived(copies_o1)
        start(copies_o2)
        arrived(copies_g1)
        start(copies_g2)
        cot_copy.wait_recv()
        zf[19 * B :, :] = jnp.zeros((16 * OWN - 19 * B, L), F32)

        arrived(copies_o2)
        flatten(GO)
        for c0, width in TILES:
            term = lax.dot_general(
                cot1_r[...], a2d[c0 : c0 + width, :], (((1,), (1,)), ((), ())), preferred_element_type=F32
            )
            for t in range(width // L):
                r0 = (c0 // L + t) * B
                zf[r0 : r0 + B, :] = term[:, t * L : (t + 1) * L]

        def flat_body(o, _):
            F16[o // 8, o % 8] = zf[pl.ds(pl.multiple_of(o * OWN, OWN), OWN), :].astype(BF16)
            return 0

        lax.fori_loop(0, 16, flat_body, 0)
        z1.start()

    @pl.when(base)
    def _():
        co_copy.wait_recv()
        GO[0, x, y] = co_r[:, :L]
        GO[1, y, x] = co_r[:, L:]
        start(copies_o1)

    arrived(copies_g2)
    flatten(GG)

    @pl.when(control)
    def _():
        z1.wait_recv()

        def pair_body(q, _):
            total = zf[pl.ds(pl.multiple_of((c * 8 + q) * OWN, OWN), OWN), :] + zr1[q].astype(F32)
            H32[q] = total
            H16[q] = total.astype(BF16)
            return 0

        lax.fori_loop(0, 8, pair_body, 0)
        start(z2)

    for i in range(2):
        hg = jnp.dot(wout[i * half : (i + 1) * half, :], a2d[...], preferred_element_type=F32)
        hidden[i * half : (i + 1) * half, :] = (hg * dgelu[i * half : (i + 1) * half, :]).astype(BF16)

    @pl.when(base)
    def _():
        arrived(copies_o1)
        start(copies_o2)

    for c0, width in TILES:
        T[c0 : c0 + width, :] = contract_rows(win[:, c0 : c0 + width], hidden[...])
    extract(sN)
    start(copies_n1)

    def stat_body(j, acc):
        at = pl.ds(pl.multiple_of(j * L, L), L)
        v = T[at, :] * cols[at, 1:2]
        xhat = (xf[at, :] - stat[0:1, :]) * stat[1:2, :]
        return acc[0] + fold(v), acc[1] + fold(v * xhat)

    p1, p2 = lax.fori_loop(0, D // L, stat_body, (zeros8, zeros8))
    st_s1[0:8, :] = p1
    st_s1[8:16, :] = p2
    start(st1)

    @pl.when(control)
    def _():
        for k in (1, 2, 3):
            z2_arrival((z + k) % 4).wait_recv()
        total = H32[pos]
        for k in (1, 2, 3):
            total = total + zr2[(z + k) % 4].astype(F32)
        A16[c, pos] = total.astype(BF16)

    @pl.when(base)
    def _():
        for k in range(4):
            z2_arrival(k).wait_recv()
        total = zr2[0].astype(F32)
        for k in (1, 2, 3):
            total = total + zr2[k].astype(F32)
        A16[c, pos] = total.astype(BF16)

    start(z3)

    arrived(copies_n1)
    rs_mid(sN, rN1, mN32, mN16)
    start(copies_n2)
    arrived(st1)
    st_s2[...] = st_s1[...] + st_r1[0] + st_r1[1] + st_r1[2]
    start(st2)

    @pl.when(base)
    def _():
        arrived(copies_o2)
        flatten(GO)
        residual = jnp.dot(zw[...], a2d[...], preferred_element_type=F32)
        block_o[...] = (rows32[...] + residual).astype(BF16)

    arrived(copies_n2)
    arrived(st2)
    rs_last(mN32, rN2, rows32)
    both = st_s2[...] + st_r2[0] + st_r2[1] + st_r2[2]
    m1 = jnp.sum(both[0:8, :], axis=0, keepdims=True) * (1.0 / D)
    m2 = jnp.sum(both[8:16, :], axis=0, keepdims=True) * (1.0 / D)
    xhat = (xf[own_rows, :] - stat[0:1, :]) * stat[1:2, :]
    ghat = rows32[...] * cols[own_rows, 1:2]
    grad_o[...] = up32[...] + stat[1:2, :] * (ghat - m1 - xhat * m2)

    arrived(z3)
    z4.start()
    z4.wait_recv()

    sent(copies_b1 + copies_b2 + copies_g1 + copies_g2 + copies_o1 + copies_o2 + copies_n1 + copies_n2)
    sent(st1 + st2 + z3 + [z4])

    @pl.when(base)
    def _():
        sent(copies_c1 + copies_c2 + [carr_copy, cot_copy])

    @pl.when(control)
    def _():
        sent(z2 + [co_copy, z1])


def finish(block, grad, flat, block_o, grad_o, zero_o, zf):
    block_o[0] = block[...]
    grad_o[0] = grad[...]

    def body(o, _):
        zf[pl.ds(pl.multiple_of(o * OWN, OWN), OWN), :] = flat[o // 8, o % 8].astype(F32)
        return 0

    lax.fori_loop(0, 16, body, 0)
    for t in range(19):
        zero_o[:, t * L : (t + 1) * L] = zf[t * B : (t + 1) * B, :]


def local(acts, modulation, w_in, w_out, zero_weight, cotangent):
    vm = pltpu.VMEM
    dma = pltpu.SemaphoreType.DMA

    def rs_bufs():
        return [vm((2, 4, 4, B, L), BF16), vm((2, 3, 4, B, L), BF16), vm((2, 4, B, L), F32), vm((2, 4, B, L), BF16), vm((2, 3, B, L), BF16)]

    scratch = [
        vm((D, N), BF16), vm((3, 1, D), F32), vm((H, D), BF16), vm((H, D), BF16), vm((B, D), BF16), vm((B, N), BF16), dma((6,)),
        vm((D, L), F32), vm((D, N), F32), vm((D, N), BF16), vm((H, N), F32), vm((H, N), F32), vm((H, N), BF16), vm((D, N), F32), vm((8, N), F32),
        *rs_bufs(), *rs_bufs(), *rs_bufs(),
        vm((2, 4, 4, B, L), BF16), vm((2, 4, 4, B, L), BF16), vm((D, N), BF16), vm((B, N), F32), vm((B, N), F32),
        vm((B, N), BF16), vm((B, N), BF16), vm((B, N), BF16), vm((B, N), BF16),
        vm((16, N), F32), vm((3, 16, N), F32), vm((16, N), F32), vm((3, 16, N), F32),
        vm((B, N), BF16), vm((16 * OWN, L), F32), vm((2, 8, OWN, L), BF16), vm((8, OWN, L), BF16), vm((8, OWN, L), F32), vm((8, OWN, L), BF16),
        vm((4, OWN, L), BF16),
        dma((10, 2, 3)), dma((10, 2, 3)), dma((2, 3)), dma((2, 3)), dma((3,)), dma((3,)), dma((2,)), dma((2,)),
        dma((7,)), dma((4,)), dma((7,)), dma((7,)),
    ]
    parts = pl.pallas_call(
        kernel,
        out_shape=(
            jax.ShapeDtypeStruct((B, N), BF16),
            jax.ShapeDtypeStruct((B, N), F32),
            jax.ShapeDtypeStruct((2, 8, OWN, L), BF16),
        ),
        in_specs=[pl.BlockSpec(memory_space=pl.ANY)] * 6,
        out_specs=[pl.BlockSpec(memory_space=pltpu.VMEM)] * 3,
        scratch_shapes=scratch,
        compiler_params=pltpu.CompilerParams(
            collective_id=0, has_side_effects=True, vmem_limit_bytes=60 * 2**20
        ),
    )(acts, jnp.transpose(modulation, (1, 0, 2)), w_in, w_out, zero_weight, cotangent)
    return pl.pallas_call(
        finish,
        out_shape=(
            jax.ShapeDtypeStruct((1, B, N), BF16),
            jax.ShapeDtypeStruct((1, B, N), F32),
            jax.ShapeDtypeStruct((B, D), F32),
        ),
        in_specs=[pl.BlockSpec(memory_space=pltpu.VMEM)] * 3,
        out_specs=[pl.BlockSpec(memory_space=pltpu.VMEM)] * 3,
        scratch_shapes=[vm((16 * OWN, L), F32)],
        compiler_params=pltpu.CompilerParams(vmem_limit_bytes=16 * 2**20),
    )(*parts)


def solution(mesh):
    placed = (
        P("grp", None, "dp"),
        P("grp", None, None),
        P("grp", "fsdp", None),
        P("grp", "fsdp", None),
        P("fsdp", None),
        P("grp", "fsdp", "dp"),
    )
    return jax.shard_map(
        local,
        mesh=mesh,
        in_specs=placed,
        out_specs=(P("grp", "fsdp", "dp"), P("grp", "fsdp", "dp"), P("fsdp", None)),
        check_vma=False,
    )
```

```python
from functools import partial

import jax
import jax.numpy as jnp
from jax import lax
from jax.experimental import pallas as pl
from jax.experimental.pallas import tpu as pltpu
from jax.sharding import PartitionSpec as P

MESH = pl.DeviceIdType.MESH
F32 = jnp.float32
BF16 = jnp.bfloat16
EPSILON = 1e-06
D = 2432
B = 152
H = 608
N = 256
L = 128
OWN = 192
GELU_C = 0.7978845608028654
TILES = ((0, 640), (640, 640), (1280, 640), (1920, 512))

C1, C2, B1, B2, G1, G2, O1, O2, N1, N2 = range(10)


def contract_rows(a, b):
    return lax.dot_general(a, b, (((0,), (0,)), ((), ())), preferred_element_type=F32)


def kernel(
    acts_h, mod_h, win_h, wout_h, zw_h, cot_h,
    block_o, grad_o, A16,
    acts, mod, win, wout, zw, cot, in_sem,
    parts, cols, xf, normed, pre, dgelu, hidden, T, stat,
    sC, rC1, mC32, mC16, rC2,
    sB, rB1, mB32, mB16, rB2,
    sN, rN1, mN32, mN16, rN2,
    GG, GO, a2d, rows32, up32,
    carr_s, carr_r, co_s, co_r,
    st_s1, st_r1, st_s2, st_r2,
    cot1_r, zf, F16, zr1, H32, H16, zr2,
    ss, rs, st_ss, st_rs, g_ss, g_rs, c_ss, c_rs, z2_ss, z2_rs, z3_ss, z3_rs,
):
    g = lax.axis_index("grp")
    f = lax.axis_index("fsdp")
    d = lax.axis_index("dp")
    y, x = f // 4, f % 4
    z, c = d // 2, d % 2
    pos = g * 4 + z
    control = g == 0
    base = g == 1

    def at_xy(py, px):
        return (g, py * 4 + px, d)

    def at_z(q):
        return (q // 4, f, (q % 4) * 2 + c)

    sibling = (g, f, z * 2 + (1 - c))
    partner = (1 - g, f, d)

    loads = [
        pltpu.make_async_copy(src, dst, in_sem.at[i])
        for i, (src, dst) in enumerate(
            ((mod_h, mod), (cot_h.at[0], cot), (zw_h, zw), (acts_h.at[0], acts), (win_h.at[0], win), (wout_h.at[0], wout))
        )
    ]
    l_mod, l_cot, l_zw, l_acts, l_win, l_wout = loads
    l_mod.start()
    l_cot.start()

    @pl.when(base)
    def _():
        l_zw.start()

    l_acts.start()
    l_win.start()

    barrier = pltpu.get_barrier_semaphore()
    for k in (1, 2, 3):
        pl.semaphore_signal(barrier, inc=1, device_id=at_xy(y, (x + k) % 4), device_id_type=MESH)
        pl.semaphore_signal(barrier, inc=1, device_id=at_xy((y + k) % 4, x), device_id_type=MESH)
    for k in range(1, 8):
        pl.semaphore_signal(barrier, inc=1, device_id=at_z((pos + k) % 8), device_id_type=MESH)
    pl.semaphore_signal(barrier, inc=1, device_id=sibling, device_id_type=MESH)

    def remote(src, dst, send, recv, where):
        return pltpu.make_async_remote_copy(
            src_ref=src, dst_ref=dst, send_sem=send, recv_sem=recv, device_id=where, device_id_type=MESH
        )

    HK = [(h, k) for k in (1, 3, 2) for h in (0, 1)]

    def peer_x(k):
        return at_xy(y, (x + k) % 4)

    def peer_y(k):
        return at_xy((y + k) % 4, x)

    def rs1(n, s, r1):
        out = []
        for h, k in HK:
            to = (x + k) % 4 if h == 0 else (y + k) % 4
            where = peer_x(k) if h == 0 else peer_y(k)
            out.append(remote(s.at[h, to], r1.at[h, k - 1], ss.at[n, h, k - 1], rs.at[n, h, k - 1], where))
        return out

    def rs2(n, m16, r2):
        out = []
        for h, k in HK:
            to = (y + k) % 4 if h == 0 else (x + k) % 4
            where = peer_y(k) if h == 0 else peer_x(k)
            out.append(remote(m16.at[h, to], r2.at[h, k - 1], ss.at[n, h, k - 1], rs.at[n, h, k - 1], where))
        return out

    def ag1(n, G):
        out = []
        for h, k in HK:
            blk = G.at[0, x, y] if h == 0 else G.at[1, y, x]
            where = peer_y(k) if h == 0 else peer_x(k)
            out.append(remote(blk, blk, ss.at[n, h, k - 1], rs.at[n, h, k - 1], where))
        return out

    def ag2(n, G):
        out = []
        for h, k in HK:
            blk = G.at[0, x] if h == 0 else G.at[1, y]
            where = peer_x(k) if h == 0 else peer_y(k)
            out.append(remote(blk, blk, ss.at[n, h, k - 1], rs.at[n, h, k - 1], where))
        return out

    def start(copies):
        for cp in copies:
            cp.start()

    def arrived(copies):
        for cp in copies:
            cp.wait_recv()

    def sent(copies):
        for cp in copies:
            cp.wait_send()

    def extract(s):
        def body(i, _):
            blk = T[pl.ds(pl.multiple_of(i * B, 8), B), :]
            s[0, i % 4, i // 4] = blk[:, :L].astype(BF16)
            s[1, i // 4, i % 4] = blk[:, L:].astype(BF16)
            return 0

        lax.fori_loop(0, 16, body, 0)

    def rs_mid(s, r1, m32, m16):
        def body(q, _):
            for h in (0, 1):
                own = x if h == 0 else y
                total = s[h, own, q].astype(F32)
                for k in range(3):
                    total = total + r1[h, k, q].astype(F32)
                m32[h, q] = total
                m16[h, q] = total.astype(BF16)
            return 0

        lax.fori_loop(0, 4, body, 0)

    def rs_last(m32, r2, out):
        for h in (0, 1):
            total = m32[h, y if h == 0 else x]
            for k in range(3):
                total = total + r2[h, k].astype(F32)
            out[:, h * L : (h + 1) * L] = total

    def flatten(G):
        def body(i, _):
            yy, xx = i // 2, 2 * (i % 2)
            rows = pl.ds(pl.multiple_of(i * 2 * B, 16), 2 * B)
            for h in (0, 1):
                p, q = (G[0, xx, yy], G[0, xx + 1, yy]) if h == 0 else (G[1, yy, xx], G[1, yy, xx + 1])
                both = jnp.concatenate([p.astype(F32), q.astype(F32)], axis=0)
                a2d[rows, h * L : (h + 1) * L] = both.astype(BF16)
            return 0

        lax.fori_loop(0, 8, body, 0)

    copies_c1, copies_c2 = rs1(C1, sC, rC1), rs2(C2, mC16, rC2)
    copies_b1, copies_b2 = rs1(B1, sB, rB1), rs2(B2, mB16, rB2)
    copies_n1, copies_n2 = rs1(N1, sN, rN1), rs2(N2, mN16, rN2)
    copies_g1, copies_g2 = ag1(G1, GG), ag2(G2, GG)
    copies_o1, copies_o2 = ag1(O1, GO), ag2(O2, GO)
    carr_copy = remote(carr_s, carr_r, g_ss.at[0], g_rs.at[0], partner)
    co_copy = remote(co_s, co_r, g_ss.at[1], g_rs.at[1], partner)
    cot_copy = remote(cot, cot1_r, g_ss.at[2], g_rs.at[2], partner)
    st1 = [remote(st_s1, st_r1.at[k - 1], st_ss.at[0, k - 1], st_rs.at[0, k - 1], peer_x(k)) for k in (1, 2, 3)]
    st2 = [remote(st_s2, st_r2.at[k - 1], st_ss.at[1, k - 1], st_rs.at[1, k - 1], peer_y(k)) for k in (1, 2, 3)]
    z1 = remote(F16.at[1 - c], zr1, c_ss.at[0], c_rs.at[0], sibling)
    z2 = [
        remote(H16.at[(pos + k) % 8], zr2.at[z], z2_ss.at[k - 1], z2_rs.at[z], at_z((pos + k) % 8))
        for k in (1, 7, 2, 6, 3, 5, 4)
    ]
    def z3_copy(i, blk, q):
        return remote(blk, blk, z3_ss.at[i], z3_rs.at[i], at_z(q % 8))

    below, above = (pos + 6) % 8, (pos + 2) % 8
    hw = OWN // 2
    near = [z3_copy(i, A16.at[c, pos], pos + by) for i, by in enumerate((1, 7, 2, 6))]
    far = [
        z3_copy(4, A16.at[c, below], pos + 1),
        z3_copy(5, A16.at[c, above], pos + 7),
        z3_copy(6, A16.at[c, below, pl.ds(0, hw)], pos + 2),
        z3_copy(7, A16.at[c, above, pl.ds(hw, hw)], pos + 6),
    ]
    z4 = [remote(A16.at[c, (pos + k) % 8], A16.at[c, (pos + k) % 8], c_ss.at[1 + k], c_rs.at[1 + k], sibling) for k in range(8)]

    def z2_arrival(zz):
        return remote(H16.at[0], zr2.at[zz], z2_ss.at[0], z2_rs.at[zz], sibling)

    l_cot.wait()

    @pl.when(base)
    def _():
        l_zw.wait()
        for c0, width in TILES:
            T[c0 : c0 + width, :] = contract_rows(zw[:, c0 : c0 + width], cot[...])
        extract(sC)

    l_mod.wait()
    row = lax.broadcasted_iota(jnp.int32, (16, L), 0)
    for j in range(D // L):
        at = slice(j * L, (j + 1) * L)
        value = jnp.zeros((16, L), F32)
        for n, m in enumerate((1.0 + mod[1, :, at], mod[0, :, at], mod[2, :, at])):
            high = m.astype(BF16).astype(F32)
            middle = (m - high).astype(BF16).astype(F32)
            for k, part in enumerate((high, middle, (m - high) - middle)):
                value = jnp.where(row == 3 * n + k, part, value)
        parts[:, at] = value.astype(BF16)
    which = lax.broadcasted_iota(jnp.int32, (16, 3 * L), 0) // 3
    column = lax.broadcasted_iota(jnp.int32, (16, 3 * L), 1) // L
    select = jnp.where(which == column, 1.0, 0.0).astype(BF16)
    for c0, width in TILES:
        cols[c0 : c0 + width, :] = contract_rows(parts[:, c0 : c0 + width], select)

    pl.semaphore_wait(barrier, 14)

    @pl.when(base)
    def _():
        start(copies_c1)
        cot_copy.start()

    def twice(v):
        return jnp.concatenate([v, v], axis=1)

    def fold(v):
        return jnp.sum(v.reshape(L // 8, 8, N), axis=0)

    l_acts.wait()
    l_wout.start()
    total = jnp.zeros((8, N), F32)
    for j in range(D // L):
        v = acts[j * L : (j + 1) * L, :].astype(F32)
        xf[j * L : (j + 1) * L, :] = v
        total = total + fold(v)
    mean = jnp.sum(total, axis=0, keepdims=True) * (1.0 / D)
    total = jnp.zeros((8, N), F32)
    for j in range(D // L):
        v = xf[j * L : (j + 1) * L, :] - mean
        total = total + fold(v * v)
    variance = jnp.sum(total, axis=0, keepdims=True) * (1.0 / D)
    rstd = lax.rsqrt(variance + EPSILON)
    stat[0:1, :] = mean
    stat[1:2, :] = rstd
    for j in range(D // L):
        at = slice(j * L, (j + 1) * L)
        v = (xf[at, :] - mean) * rstd
        normed[at, :] = (v * twice(cols[at, :L]) + twice(cols[at, L : 2 * L])).astype(BF16)

    l_win.wait()
    half = H // 2
    for i in range(2):
        pre[i * half : (i + 1) * half, :] = jnp.dot(
            win[i * half : (i + 1) * half, :], normed[...], preferred_element_type=F32
        )

    def gelu_body(j, _):
        at = pl.ds(pl.multiple_of(j * 32, 32), 32)
        v = pre[at, :]
        v2 = v * v
        t = jnp.tanh(GELU_C * (v + 0.044715 * (v2 * v)))
        cdf = 0.5 * (1.0 + t)
        hidden[at, :] = (v * cdf).astype(BF16)
        dgelu[at, :] = cdf + 0.5 * v * (1.0 - t * t) * (GELU_C * (1.0 + 3.0 * 0.044715 * v2))
        return 0

    lax.fori_loop(0, H // 32, gelu_body, 0)
    l_wout.wait()

    def produce(n, weights, s, r1, send):
        for yy, (c0, width) in enumerate(TILES):
            T[c0 : c0 + width, :] = contract_rows(weights[:, c0 : c0 + width], hidden[...])
            for xx in range(4):
                blk = T[(yy * 4 + xx) * B : (yy * 4 + xx + 1) * B, :]
                s[0, xx, yy] = blk[:, :L].astype(BF16)
                s[1, yy, xx] = blk[:, L:].astype(BF16)

            @pl.when(send)
            def _():
                for k in (1, 3, 2):
                    to = (x + k) % 4
                    remote(
                        s.at[0, to, yy], r1.at[0, k - 1, yy], ss.at[n, 0, k - 1], rs.at[n, 0, k - 1], peer_x(k)
                    ).start()

            @pl.when(jnp.logical_and(send, y != yy))
            def _():
                k = (yy + 4 - y) % 4
                remote(
                    s.at[1, yy], r1.at[1, k - 1], ss.at[n, 1, k - 1], rs.at[n, 1, k - 1], at_xy(yy, x)
                ).start()

    produce(B1, wout, sB, rB1, control)

    own_rows = pl.ds(pl.multiple_of(f * B, 8), B)
    gate_rows = twice(cols[own_rows, 2 * L :])

    def set_gate_grad(up):
        gg = (gate_rows * up).astype(BF16)
        GG[0, x, y] = gg[:, :L]
        GG[1, y, x] = gg[:, L:]

    @pl.when(base)
    def _():
        arrived(copies_c1)
        rs_mid(sC, rC1, mC32, mC16)
        start(copies_c2)
        up = cot[...].astype(F32)
        up32[...] = up
        set_gate_grad(up)
        start(copies_g1)
        arrived(copies_c2)
        rs_last(mC32, rC2, rows32)
        carr_s[...] = rows32[...].astype(BF16)
        carr_copy.start()
        start(copies_b1)
        arrived(copies_g1)
        start(copies_g2)

    arrived(copies_b1)
    rs_mid(sB, rB1, mB32, mB16)
    start(copies_b2)
    arrived(copies_b2)
    rs_last(mB32, rB2, rows32)
    rows32[...] = xf[own_rows, :] + gate_rows * rows32[...]

    @pl.when(control)
    def _():
        out = rows32[...].astype(BF16)
        block_o[...] = out
        co_s[...] = out
        co_copy.start()
        GO[0, x, y] = out[:, :L]
        GO[1, y, x] = out[:, L:]
        start(copies_o1)
        carr_copy.wait_recv()
        up = carr_r[...].astype(F32) + cot[...].astype(F32)
        up32[...] = up
        set_gate_grad(up)
        start(copies_g1)
        arrived(copies_o1)
        start(copies_o2)
        cot_copy.wait_recv()
        zf[19 * B :, :] = jnp.zeros((16 * OWN - 19 * B, L), F32)

        arrived(copies_o2)
        arrived(copies_g1)
        start(copies_g2)
        flatten(GO)
        for c0, width in TILES:
            term = lax.dot_general(
                cot1_r[...], a2d[c0 : c0 + width, :], (((1,), (1,)), ((), ())), preferred_element_type=F32
            )
            for t in range(width // L):
                r0 = (c0 // L + t) * B
                zf[r0 : r0 + B, :] = term[:, t * L : (t + 1) * L]

        def flat_body(o, _):
            F16[o // 8, o % 8] = zf[pl.ds(pl.multiple_of(o * OWN, OWN), OWN), :].astype(BF16)
            return 0

        lax.fori_loop(0, 16, flat_body, 0)
        z1.start()

    @pl.when(base)
    def _():
        co_copy.wait_recv()
        GO[0, x, y] = co_r[:, :L]
        GO[1, y, x] = co_r[:, L:]
        start(copies_o1)

    @pl.when(control)
    def _():
        z1.wait_recv()

        def pair_body(q, _):
            total = zf[pl.ds(pl.multiple_of((c * 8 + q) * OWN, OWN), OWN), :] + zr1[q].astype(F32)
            H32[q] = total
            H16[q] = total.astype(BF16)
            return 0

        lax.fori_loop(0, 8, pair_body, 0)
        start(z2)

    arrived(copies_g2)
    flatten(GG)
    for i in range(2):
        hg = jnp.dot(wout[i * half : (i + 1) * half, :], a2d[...], preferred_element_type=F32)
        hidden[i * half : (i + 1) * half, :] = (hg * dgelu[i * half : (i + 1) * half, :]).astype(BF16)

    @pl.when(base)
    def _():
        arrived(copies_o1)
        start(copies_o2)

    produce(N1, win, sN, rN1, g >= 0)
    p1 = jnp.zeros((8, N), F32)
    p2 = jnp.zeros((8, N), F32)
    for j in range(D // L):
        at = slice(j * L, (j + 1) * L)
        v = T[at, :] * twice(cols[at, :L])
        p1 = p1 + fold(v)
        p2 = p2 + fold(v * ((xf[at, :] - stat[0:1, :]) * stat[1:2, :]))
    st_s1[0:8, :] = p1
    st_s1[8:16, :] = p2
    start(st1)

    @pl.when(control)
    def _():
        for k in (1, 2, 3):
            z2_arrival((z + k) % 4).wait_recv()
        total = H32[pos]
        for k in (1, 2, 3):
            total = total + zr2[(z + k) % 4].astype(F32)
        A16[c, pos] = total.astype(BF16)

    @pl.when(base)
    def _():
        for k in range(4):
            z2_arrival(k).wait_recv()
        total = zr2[0].astype(F32)
        for k in (1, 2, 3):
            total = total + zr2[k].astype(F32)
        A16[c, pos] = total.astype(BF16)

    start(near)
    z4[0].start()

    arrived(copies_n1)
    rs_mid(sN, rN1, mN32, mN16)
    start(copies_n2)
    arrived(st1)
    st_s2[...] = st_s1[...] + st_r1[0] + st_r1[1] + st_r1[2]
    start(st2)

    @pl.when(base)
    def _():
        arrived(copies_o2)
        flatten(GO)
        residual = jnp.dot(zw[...], a2d[...], preferred_element_type=F32)
        block_o[...] = (rows32[...] + residual).astype(BF16)

    arrived(near)
    start(far)
    start(z4[1:3] + z4[6:8])
    arrived(copies_n2)
    arrived(st2)
    rs_last(mN32, rN2, rows32)
    both = st_s2[...] + st_r2[0] + st_r2[1] + st_r2[2]
    m1 = jnp.sum(both[0:8, :], axis=0, keepdims=True) * (1.0 / D)
    m2 = jnp.sum(both[8:16, :], axis=0, keepdims=True) * (1.0 / D)
    xhat = (xf[own_rows, :] - stat[0:1, :]) * stat[1:2, :]
    ghat = rows32[...] * twice(cols[own_rows, :L])
    grad_o[...] = up32[...] + stat[1:2, :] * (ghat - m1 - xhat * m2)

    arrived(far)
    start(z4[3:6])
    arrived(z4)

    sent(copies_b1 + copies_b2 + copies_g1 + copies_g2 + copies_o1 + copies_o2 + copies_n1 + copies_n2)
    sent(st1 + st2 + near + far + z4)

    @pl.when(base)
    def _():
        sent(copies_c1 + copies_c2 + [carr_copy, cot_copy])

    @pl.when(control)
    def _():
        sent(z2 + [co_copy, z1])


def finish(block, grad, flat, block_o, grad_o, zero_o, flat_v, zf, rows, sem):
    copies = [
        pltpu.make_async_copy(flat, flat_v, sem.at[0]),
        pltpu.make_async_copy(block, block_o.at[0], sem.at[1]),
        pltpu.make_async_copy(grad, grad_o.at[0], sem.at[2]),
    ]
    for cp in copies:
        cp.start()
    copies[0].wait()

    def body(o, _):
        zf[pl.ds(pl.multiple_of(o * OWN, OWN), OWN), :] = flat_v[o // 8, o % 8].astype(F32)
        return 0

    lax.fori_loop(0, 16, body, 0)
    for t in range(19):
        rows[:, t * L : (t + 1) * L] = zf[t * B : (t + 1) * B, :]
    out = pltpu.make_async_copy(rows, zero_o, sem.at[3])
    out.start()
    out.wait()
    copies[1].wait()
    copies[2].wait()


def local(acts, modulation, w_in, w_out, zero_weight, cotangent):
    vm = pltpu.VMEM
    dma = pltpu.SemaphoreType.DMA

    def rs_bufs():
        return [vm((2, 4, 4, B, L), BF16), vm((2, 3, 4, B, L), BF16), vm((2, 4, B, L), F32), vm((2, 4, B, L), BF16), vm((2, 3, B, L), BF16)]

    scratch = [
        vm((D, N), BF16), vm((3, 1, D), F32), vm((H, D), BF16), vm((H, D), BF16), vm((B, D), BF16), vm((B, N), BF16), dma((6,)),
        vm((16, D), BF16), vm((D, 3 * L), F32), vm((D, N), F32), vm((D, N), BF16), vm((H, N), F32), vm((H, N), F32), vm((H, N), BF16), vm((D, N), F32), vm((8, N), F32),
        *rs_bufs(), *rs_bufs(), *rs_bufs(),
        vm((2, 4, 4, B, L), BF16), vm((2, 4, 4, B, L), BF16), vm((D, N), BF16), vm((B, N), F32), vm((B, N), F32),
        vm((B, N), BF16), vm((B, N), BF16), vm((B, N), BF16), vm((B, N), BF16),
        vm((16, N), F32), vm((3, 16, N), F32), vm((16, N), F32), vm((3, 16, N), F32),
        vm((B, N), BF16), vm((16 * OWN, L), F32), vm((2, 8, OWN, L), BF16), vm((8, OWN, L), BF16), vm((8, OWN, L), F32), vm((8, OWN, L), BF16),
        vm((4, OWN, L), BF16),
        dma((10, 2, 3)), dma((10, 2, 3)), dma((2, 3)), dma((2, 3)), dma((3,)), dma((3,)), dma((9,)), dma((9,)),
        dma((7,)), dma((4,)), dma((8,)), dma((8,)),
    ]
    results = pl.pallas_call(
        kernel,
        out_shape=(
            jax.ShapeDtypeStruct((B, N), BF16),
            jax.ShapeDtypeStruct((B, N), F32),
            jax.ShapeDtypeStruct((2, 8, OWN, L), BF16),
        ),
        in_specs=[pl.BlockSpec(memory_space=pl.ANY)] * 6,
        out_specs=[pl.BlockSpec(memory_space=pltpu.VMEM)] * 3,
        scratch_shapes=scratch,
        compiler_params=pltpu.CompilerParams(
            collective_id=0, has_side_effects=True, vmem_limit_bytes=60 * 2**20
        ),
    )(acts, jnp.transpose(modulation, (1, 0, 2)), w_in, w_out, zero_weight, cotangent)
    return pl.pallas_call(
        finish,
        out_shape=(
            jax.ShapeDtypeStruct((1, B, N), BF16),
            jax.ShapeDtypeStruct((1, B, N), F32),
            jax.ShapeDtypeStruct((B, D), F32),
        ),
        in_specs=[pl.BlockSpec(memory_space=pl.ANY)] * 3,
        out_specs=[pl.BlockSpec(memory_space=pl.ANY)] * 3,
        scratch_shapes=[vm((2, 8, OWN, L), BF16), vm((16 * OWN, L), F32), vm((B, D), F32), dma((4,))],
        compiler_params=pltpu.CompilerParams(vmem_limit_bytes=60 * 2**20),
    )(*results)


def solution(mesh):
    placed = (
        P("grp", None, "dp"),
        P("grp", None, None),
        P("grp", "fsdp", None),
        P("grp", "fsdp", None),
        P("fsdp", None),
        P("grp", "fsdp", "dp"),
    )
    return jax.shard_map(
        local,
        mesh=mesh,
        in_specs=placed,
        out_specs=(P("grp", "fsdp", "dp"), P("grp", "fsdp", "dp"), P("fsdp", None)),
        check_vma=False,
    )
```

```python
from functools import partial

import jax
import jax.numpy as jnp
from jax import lax
from jax.experimental import pallas as pl
from jax.experimental.pallas import tpu as pltpu
from jax.sharding import PartitionSpec as P

MESH = pl.DeviceIdType.MESH
F32 = jnp.float32
BF16 = jnp.bfloat16
EPSILON = 1e-06
D = 2432
B = 152
H = 608
N = 256
L = 128
OWN = 96
GELU_C = 0.7978845608028654
TILES = ((0, 640), (640, 640), (1280, 640), (1920, 512))

C1, C2, B1, B2, G1, G2, O1, O2, N1, N2 = range(10)


def contract_rows(a, b):
    return lax.dot_general(a, b, (((0,), (0,)), ((), ())), preferred_element_type=F32)


def kernel(
    acts_h, mod_h, win_h, wout_h, zw_h, cot_h,
    block_o, grad_o, A16,
    acts, mod, win, wout, zw, cot, in_sem,
    parts, cols, xf, normed, pre, dgelu, hidden, T, stat,
    sC, rC1, mC32, mC16, rC2,
    sB, rB1, mB32, mB16, rB2,
    sN, rN1, mN32, mN16, rN2,
    GG, GO, a2d, rows32, up32,
    carr_s, carr_r, co_s, co_r,
    st_s1, st_r1, st_s2, st_r2,
    cot1_r, zf, F16, zr1, H32, H16, zr2,
    ss, rs, st_ss, st_rs, g_ss, g_rs, c_ss, c_rs, z2_ss, z2_rs, z3_ss, z3_rs, z4_ss, z4_rs,
):
    g = lax.axis_index("grp")
    f = lax.axis_index("fsdp")
    d = lax.axis_index("dp")
    y, x = f // 4, f % 4
    z, c = d // 2, d % 2
    pos = g * 4 + z
    control = g == 0
    base = g == 1

    def at_xy(py, px):
        return (g, py * 4 + px, d)

    def at_z(q):
        return (q // 4, f, (q % 4) * 2 + c)

    sibling = (g, f, z * 2 + (1 - c))
    partner = (1 - g, f, d)

    loads = [
        pltpu.make_async_copy(src, dst, in_sem.at[i])
        for i, (src, dst) in enumerate(
            ((mod_h, mod), (cot_h.at[0], cot), (zw_h, zw), (acts_h.at[0], acts), (win_h.at[0], win), (wout_h.at[0], wout))
        )
    ]
    l_mod, l_cot, l_zw, l_acts, l_win, l_wout = loads
    l_mod.start()
    l_cot.start()

    @pl.when(base)
    def _():
        l_zw.start()

    l_acts.start()
    l_win.start()

    barrier = pltpu.get_barrier_semaphore()
    for k in (1, 2, 3):
        pl.semaphore_signal(barrier, inc=1, device_id=at_xy(y, (x + k) % 4), device_id_type=MESH)
        pl.semaphore_signal(barrier, inc=1, device_id=at_xy((y + k) % 4, x), device_id_type=MESH)
    for k in range(1, 8):
        pl.semaphore_signal(barrier, inc=1, device_id=at_z((pos + k) % 8), device_id_type=MESH)
    pl.semaphore_signal(barrier, inc=1, device_id=sibling, device_id_type=MESH)

    def remote(src, dst, send, recv, where):
        return pltpu.make_async_remote_copy(
            src_ref=src, dst_ref=dst, send_sem=send, recv_sem=recv, device_id=where, device_id_type=MESH
        )

    HK = [(h, k) for k in (1, 3, 2) for h in (0, 1)]

    def peer_x(k):
        return at_xy(y, (x + k) % 4)

    def peer_y(k):
        return at_xy((y + k) % 4, x)

    def rs1(n, s, r1):
        out = []
        for h, k in HK:
            to = (x + k) % 4 if h == 0 else (y + k) % 4
            where = peer_x(k) if h == 0 else peer_y(k)
            out.append(remote(s.at[h, to], r1.at[h, k - 1], ss.at[n, h, k - 1], rs.at[n, h, k - 1], where))
        return out

    def rs2(n, m16, r2):
        out = []
        for h, k in HK:
            to = (y + k) % 4 if h == 0 else (x + k) % 4
            where = peer_y(k) if h == 0 else peer_x(k)
            out.append(remote(m16.at[h, to], r2.at[h, k - 1], ss.at[n, h, k - 1], rs.at[n, h, k - 1], where))
        return out

    def ag1(n, G):
        out = []
        for h, k in HK:
            blk = G.at[0, x, y] if h == 0 else G.at[1, y, x]
            where = peer_y(k) if h == 0 else peer_x(k)
            out.append(remote(blk, blk, ss.at[n, h, k - 1], rs.at[n, h, k - 1], where))
        return out

    def ag2(n, G):
        out = []
        for h, k in HK:
            blk = G.at[0, x] if h == 0 else G.at[1, y]
            where = peer_x(k) if h == 0 else peer_y(k)
            out.append(remote(blk, blk, ss.at[n, h, k - 1], rs.at[n, h, k - 1], where))
        return out

    def start(copies):
        for cp in copies:
            cp.start()

    def arrived(copies):
        for cp in copies:
            cp.wait_recv()

    def sent(copies):
        for cp in copies:
            cp.wait_send()

    def extract(s):
        def body(i, _):
            blk = T[pl.ds(pl.multiple_of(i * B, 8), B), :]
            s[0, i % 4, i // 4] = blk[:, :L].astype(BF16)
            s[1, i // 4, i % 4] = blk[:, L:].astype(BF16)
            return 0

        lax.fori_loop(0, 16, body, 0)

    def rs_mid(s, r1, m32, m16):
        def body(q, _):
            for h in (0, 1):
                own = x if h == 0 else y
                total = s[h, own, q].astype(F32)
                for k in range(3):
                    total = total + r1[h, k, q].astype(F32)
                m32[h, q] = total
                m16[h, q] = total.astype(BF16)
            return 0

        lax.fori_loop(0, 4, body, 0)

    def rs_last(m32, r2, out):
        for h in (0, 1):
            total = m32[h, y if h == 0 else x]
            for k in range(3):
                total = total + r2[h, k].astype(F32)
            out[:, h * L : (h + 1) * L] = total

    def flatten(G):
        def body(i, _):
            yy, xx = i // 2, 2 * (i % 2)
            rows = pl.ds(pl.multiple_of(i * 2 * B, 16), 2 * B)
            for h in (0, 1):
                p, q = (G[0, xx, yy], G[0, xx + 1, yy]) if h == 0 else (G[1, yy, xx], G[1, yy, xx + 1])
                both = jnp.concatenate([p.astype(F32), q.astype(F32)], axis=0)
                a2d[rows, h * L : (h + 1) * L] = both.astype(BF16)
            return 0

        lax.fori_loop(0, 8, body, 0)

    copies_c1, copies_c2 = rs1(C1, sC, rC1), rs2(C2, mC16, rC2)
    copies_b1, copies_b2 = rs1(B1, sB, rB1), rs2(B2, mB16, rB2)
    copies_n1, copies_n2 = rs1(N1, sN, rN1), rs2(N2, mN16, rN2)
    copies_g1, copies_g2 = ag1(G1, GG), ag2(G2, GG)
    copies_o1, copies_o2 = ag1(O1, GO), ag2(O2, GO)
    carr_copy = remote(carr_s, carr_r, g_ss.at[0], g_rs.at[0], partner)
    co_copy = remote(co_s, co_r, g_ss.at[1], g_rs.at[1], partner)
    cot_copy = remote(cot, cot1_r, g_ss.at[2], g_rs.at[2], partner)
    st1 = [remote(st_s1, st_r1.at[k - 1], st_ss.at[0, k - 1], st_rs.at[0, k - 1], peer_x(k)) for k in (1, 2, 3)]
    st2 = [remote(st_s2, st_r2.at[k - 1], st_ss.at[1, k - 1], st_rs.at[1, k - 1], peer_y(k)) for k in (1, 2, 3)]
    z1 = [remote(F16.at[e, 1 - c], zr1.at[e], c_ss.at[e], c_rs.at[e], sibling) for e in (0, 1)]
    z2 = [
        [
            remote(
                H16.at[e, (pos + k) % 8], zr2.at[e, z], z2_ss.at[e, k - 1], z2_rs.at[e, z], at_z((pos + k) % 8)
            )
            for k in (1, 7, 2, 6, 3, 5, 4)
        ]
        for e in (0, 1)
    ]

    def z3_copy(e, i, blk, q):
        return remote(blk, blk, z3_ss.at[e, i], z3_rs.at[e, i], at_z(q % 8))

    below, above = (pos + 6) % 8, (pos + 2) % 8
    hw = OWN // 2
    near = [[z3_copy(e, i, A16.at[e, c, pos], pos + by) for i, by in enumerate((1, 7, 2, 6))] for e in (0, 1)]
    far = [
        [
            z3_copy(e, 4, A16.at[e, c, below], pos + 1),
            z3_copy(e, 5, A16.at[e, c, above], pos + 7),
            z3_copy(e, 6, A16.at[e, c, below, pl.ds(0, hw)], pos + 2),
            z3_copy(e, 7, A16.at[e, c, above, pl.ds(hw, hw)], pos + 6),
        ]
        for e in (0, 1)
    ]
    z4 = [
        [
            remote(
                A16.at[e, c, (pos + k) % 8], A16.at[e, c, (pos + k) % 8], z4_ss.at[e, k], z4_rs.at[e, k], sibling
            )
            for k in range(8)
        ]
        for e in (0, 1)
    ]

    def z2_arrival(e, zz):
        return remote(H16.at[e, 0], zr2.at[e, zz], z2_ss.at[e, 0], z2_rs.at[e, zz], sibling)

    l_cot.wait()

    @pl.when(base)
    def _():
        l_zw.wait()
        for c0, width in TILES:
            T[c0 : c0 + width, :] = contract_rows(zw[:, c0 : c0 + width], cot[...])
        extract(sC)

    pl.semaphore_wait(barrier, 14)

    @pl.when(base)
    def _():
        start(copies_c1)
        cot_copy.start()

    l_mod.wait()
    row = lax.broadcasted_iota(jnp.int32, (16, L), 0)
    for j in range(D // L):
        at = slice(j * L, (j + 1) * L)
        value = jnp.zeros((16, L), F32)
        for n, m in enumerate((1.0 + mod[1, :, at], mod[0, :, at], mod[2, :, at])):
            high = m.astype(BF16).astype(F32)
            middle = (m - high).astype(BF16).astype(F32)
            for k, part in enumerate((high, middle, (m - high) - middle)):
                value = jnp.where(row == 3 * n + k, part, value)
        parts[:, at] = value.astype(BF16)
    which = lax.broadcasted_iota(jnp.int32, (16, 3 * L), 0) // 3
    column = lax.broadcasted_iota(jnp.int32, (16, 3 * L), 1) // L
    select = jnp.where(which == column, 1.0, 0.0).astype(BF16)
    for c0, width in TILES:
        cols[c0 : c0 + width, :] = contract_rows(parts[:, c0 : c0 + width], select)

    def twice(v):
        return jnp.concatenate([v, v], axis=1)

    def fold(v):
        return jnp.sum(v.reshape(L // 8, 8, N), axis=0)

    l_acts.wait()
    l_wout.start()
    total = jnp.zeros((8, N), F32)
    for j in range(D // L):
        v = acts[j * L : (j + 1) * L, :].astype(F32)
        xf[j * L : (j + 1) * L, :] = v
        total = total + fold(v)
    mean = jnp.sum(total, axis=0, keepdims=True) * (1.0 / D)
    total = jnp.zeros((8, N), F32)
    for j in range(D // L):
        v = xf[j * L : (j + 1) * L, :] - mean
        total = total + fold(v * v)
    variance = jnp.sum(total, axis=0, keepdims=True) * (1.0 / D)
    rstd = lax.rsqrt(variance + EPSILON)
    stat[0:1, :] = mean
    stat[1:2, :] = rstd
    for j in range(D // L):
        at = slice(j * L, (j + 1) * L)
        v = (xf[at, :] - mean) * rstd
        normed[at, :] = (v * twice(cols[at, :L]) + twice(cols[at, L : 2 * L])).astype(BF16)

    l_win.wait()
    half = H // 2
    for i in range(2):
        pre[i * half : (i + 1) * half, :] = jnp.dot(
            win[i * half : (i + 1) * half, :], normed[...], preferred_element_type=F32
        )

    def gelu_body(j, _):
        at = pl.ds(pl.multiple_of(j * 32, 32), 32)
        v = pre[at, :]
        v2 = v * v
        t = jnp.tanh(GELU_C * (v + 0.044715 * (v2 * v)))
        cdf = 0.5 * (1.0 + t)
        hidden[at, :] = (v * cdf).astype(BF16)
        dgelu[at, :] = cdf + 0.5 * v * (1.0 - t * t) * (GELU_C * (1.0 + 3.0 * 0.044715 * v2))
        return 0

    lax.fori_loop(0, H // 32, gelu_body, 0)
    l_wout.wait()

    def produce(n, weights, s, r1, send):
        for yy, (c0, width) in enumerate(TILES):
            T[c0 : c0 + width, :] = contract_rows(weights[:, c0 : c0 + width], hidden[...])
            for xx in range(4):
                blk = T[(yy * 4 + xx) * B : (yy * 4 + xx + 1) * B, :]
                s[0, xx, yy] = blk[:, :L].astype(BF16)
                s[1, yy, xx] = blk[:, L:].astype(BF16)

            @pl.when(send)
            def _():
                for k in (1, 3, 2):
                    to = (x + k) % 4
                    remote(
                        s.at[0, to, yy], r1.at[0, k - 1, yy], ss.at[n, 0, k - 1], rs.at[n, 0, k - 1], peer_x(k)
                    ).start()

            @pl.when(jnp.logical_and(send, y != yy))
            def _():
                k = (yy + 4 - y) % 4
                remote(
                    s.at[1, yy], r1.at[1, k - 1], ss.at[n, 1, k - 1], rs.at[n, 1, k - 1], at_xy(yy, x)
                ).start()

    produce(B1, wout, sB, rB1, control)

    own_rows = pl.ds(pl.multiple_of(f * B, 8), B)
    gate_rows = twice(cols[own_rows, 2 * L :])

    def set_gate_grad(up):
        gg = (gate_rows * up).astype(BF16)
        GG[0, x, y] = gg[:, :L]
        GG[1, y, x] = gg[:, L:]

    @pl.when(base)
    def _():
        arrived(copies_c1)
        rs_mid(sC, rC1, mC32, mC16)
        start(copies_c2)
        up = cot[...].astype(F32)
        up32[...] = up
        set_gate_grad(up)
        start(copies_g1)
        arrived(copies_c2)
        rs_last(mC32, rC2, rows32)
        carr_s[...] = rows32[...].astype(BF16)
        carr_copy.start()
        start(copies_b1)
        arrived(copies_g1)
        start(copies_g2)

    arrived(copies_b1)
    rs_mid(sB, rB1, mB32, mB16)
    start(copies_b2)
    arrived(copies_b2)
    rs_last(mB32, rB2, rows32)
    rows32[...] = xf[own_rows, :] + gate_rows * rows32[...]

    @pl.when(control)
    def _():
        out = rows32[...].astype(BF16)
        block_o[...] = out
        co_s[...] = out
        co_copy.start()
        GO[0, x, y] = out[:, :L]
        GO[1, y, x] = out[:, L:]
        start(copies_o1)
        carr_copy.wait_recv()
        up = carr_r[...].astype(F32) + cot[...].astype(F32)
        up32[...] = up
        set_gate_grad(up)
        start(copies_g1)
        arrived(copies_o1)
        start(copies_o2)
        cot_copy.wait_recv()
        zf[19 * B :, :] = jnp.zeros((32 * OWN - 19 * B, L), F32)

        arrived(copies_o2)
        arrived(copies_g1)
        start(copies_g2)
        flatten(GO)
        for c0, width in TILES:
            term = lax.dot_general(
                cot1_r[...], a2d[c0 : c0 + width, :], (((1,), (1,)), ((), ())), preferred_element_type=F32
            )
            for t in range(width // L):
                r0 = (c0 // L + t) * B
                zf[r0 : r0 + B, :] = term[:, t * L : (t + 1) * L]

        for e in (0, 1):

            def flat_body(o, _):
                at = pl.ds(pl.multiple_of((e * 16 + o) * OWN, OWN), OWN)
                F16[e, o // 8, o % 8] = zf[at, :].astype(BF16)
                return 0

            lax.fori_loop(0, 16, flat_body, 0)
            z1[e].start()

    @pl.when(base)
    def _():
        co_copy.wait_recv()
        GO[0, x, y] = co_r[:, :L]
        GO[1, y, x] = co_r[:, L:]
        start(copies_o1)

    @pl.when(control)
    def _():
        for e in (0, 1):
            z1[e].wait_recv()

            def pair_body(q, _):
                at = pl.ds(pl.multiple_of((e * 16 + c * 8 + q) * OWN, OWN), OWN)
                total = zf[at, :] + zr1[e, q].astype(F32)
                H32[e, q] = total
                H16[e, q] = total.astype(BF16)
                return 0

            lax.fori_loop(0, 8, pair_body, 0)
            start(z2[e])

    arrived(copies_g2)
    flatten(GG)
    for i in range(2):
        hg = jnp.dot(wout[i * half : (i + 1) * half, :], a2d[...], preferred_element_type=F32)
        hidden[i * half : (i + 1) * half, :] = (hg * dgelu[i * half : (i + 1) * half, :]).astype(BF16)

    @pl.when(base)
    def _():
        arrived(copies_o1)
        start(copies_o2)

    produce(N1, win, sN, rN1, g >= 0)
    p1 = jnp.zeros((8, N), F32)
    p2 = jnp.zeros((8, N), F32)
    for j in range(D // L):
        at = slice(j * L, (j + 1) * L)
        v = T[at, :] * twice(cols[at, :L])
        p1 = p1 + fold(v)
        p2 = p2 + fold(v * ((xf[at, :] - stat[0:1, :]) * stat[1:2, :]))
    st_s1[0:8, :] = p1
    st_s1[8:16, :] = p2
    start(st1)

    for e in (0, 1):

        @pl.when(control)
        def _():
            for k in (1, 2, 3):
                z2_arrival(e, (z + k) % 4).wait_recv()
            total = H32[e, pos]
            for k in (1, 2, 3):
                total = total + zr2[e, (z + k) % 4].astype(F32)
            A16[e, c, pos] = total.astype(BF16)

        @pl.when(base)
        def _():
            for k in range(4):
                z2_arrival(e, k).wait_recv()
            total = zr2[e, 0].astype(F32)
            for k in (1, 2, 3):
                total = total + zr2[e, k].astype(F32)
            A16[e, c, pos] = total.astype(BF16)

        start(near[e])
        z4[e][0].start()

    def pass_on(e):
        arrived(near[e])
        start(far[e])
        start(z4[e][1:3] + z4[e][6:8])

    pass_on(0)

    arrived(copies_n1)
    rs_mid(sN, rN1, mN32, mN16)
    start(copies_n2)
    arrived(st1)
    st_s2[...] = st_s1[...] + st_r1[0] + st_r1[1] + st_r1[2]
    start(st2)
    pass_on(1)

    @pl.when(base)
    def _():
        arrived(copies_o2)
        flatten(GO)
        residual = jnp.dot(zw[...], a2d[...], preferred_element_type=F32)
        block_o[...] = (rows32[...] + residual).astype(BF16)

    arrived(copies_n2)
    arrived(st2)
    rs_last(mN32, rN2, rows32)
    both = st_s2[...] + st_r2[0] + st_r2[1] + st_r2[2]
    m1 = jnp.sum(both[0:8, :], axis=0, keepdims=True) * (1.0 / D)
    m2 = jnp.sum(both[8:16, :], axis=0, keepdims=True) * (1.0 / D)
    xhat = (xf[own_rows, :] - stat[0:1, :]) * stat[1:2, :]
    ghat = rows32[...] * twice(cols[own_rows, :L])
    grad_o[...] = up32[...] + stat[1:2, :] * (ghat - m1 - xhat * m2)

    for e in (0, 1):
        arrived(far[e])
        start(z4[e][3:6])
    arrived(z4[0] + z4[1])

    sent(copies_b1 + copies_b2 + copies_g1 + copies_g2 + copies_o1 + copies_o2 + copies_n1 + copies_n2)
    sent(st1 + st2 + near[0] + near[1] + far[0] + far[1] + z4[0] + z4[1])

    @pl.when(base)
    def _():
        sent(copies_c1 + copies_c2 + [carr_copy, cot_copy])

    @pl.when(control)
    def _():
        sent(z2[0] + z2[1] + z1 + [co_copy])


def finish(block, grad, flat, block_o, grad_o, zero_o, flat_v, zf, rows, block_v, grad_v, sem):
    def move(src, dst, i):
        cp = pltpu.make_async_copy(src, dst, sem.at[i])
        cp.start()
        return cp

    ins = [move(flat, flat_v, 0), move(grad, grad_v, 1), move(block, block_v, 2)]
    ins[1].wait()
    outs = [move(grad_v, grad_o.at[0], 3)]
    ins[2].wait()
    outs.append(move(block_v, block_o.at[0], 4))
    ins[0].wait()
    for o in range(32):
        zf[o * OWN : (o + 1) * OWN, :] = flat_v[o // 16, (o // 8) % 2, o % 8].astype(F32)
    for t in range(19):
        rows[:, t * L : (t + 1) * L] = zf[t * B : (t + 1) * B, :]
    outs.append(move(rows, zero_o, 5))
    for cp in outs:
        cp.wait()


def local(acts, modulation, w_in, w_out, zero_weight, cotangent):
    vm = pltpu.VMEM
    dma = pltpu.SemaphoreType.DMA

    def rs_bufs():
        return [vm((2, 4, 4, B, L), BF16), vm((2, 3, 4, B, L), BF16), vm((2, 4, B, L), F32), vm((2, 4, B, L), BF16), vm((2, 3, B, L), BF16)]

    scratch = [
        vm((D, N), BF16), vm((3, 1, D), F32), vm((H, D), BF16), vm((H, D), BF16), vm((B, D), BF16), vm((B, N), BF16), dma((6,)),
        vm((16, D), BF16), vm((D, 3 * L), F32), vm((D, N), F32), vm((D, N), BF16), vm((H, N), F32), vm((H, N), F32), vm((H, N), BF16), vm((D, N), F32), vm((8, N), F32),
        *rs_bufs(), *rs_bufs(), *rs_bufs(),
        vm((2, 4, 4, B, L), BF16), vm((2, 4, 4, B, L), BF16), vm((D, N), BF16), vm((B, N), F32), vm((B, N), F32),
        vm((B, N), BF16), vm((B, N), BF16), vm((B, N), BF16), vm((B, N), BF16),
        vm((16, N), F32), vm((3, 16, N), F32), vm((16, N), F32), vm((3, 16, N), F32),
        vm((B, N), BF16), vm((32 * OWN, L), F32), vm((2, 2, 8, OWN, L), BF16), vm((2, 8, OWN, L), BF16), vm((2, 8, OWN, L), F32),
        vm((2, 8, OWN, L), BF16), vm((2, 4, OWN, L), BF16),
        dma((10, 2, 3)), dma((10, 2, 3)), dma((2, 3)), dma((2, 3)), dma((3,)), dma((3,)), dma((2,)), dma((2,)),
        dma((2, 7)), dma((2, 4)), dma((2, 8)), dma((2, 8)), dma((2, 8)), dma((2, 8)),
    ]
    results = pl.pallas_call(
        kernel,
        out_shape=(
            jax.ShapeDtypeStruct((B, N), BF16),
            jax.ShapeDtypeStruct((B, N), F32),
            jax.ShapeDtypeStruct((2, 2, 8, OWN, L), BF16),
        ),
        in_specs=[pl.BlockSpec(memory_space=pl.ANY)] * 6,
        out_specs=[pl.BlockSpec(memory_space=pltpu.VMEM)] * 3,
        scratch_shapes=scratch,
        compiler_params=pltpu.CompilerParams(
            collective_id=0, has_side_effects=True, vmem_limit_bytes=60 * 2**20
        ),
    )(acts, jnp.transpose(modulation, (1, 0, 2)), w_in, w_out, zero_weight, cotangent)
    return pl.pallas_call(
        finish,
        out_shape=(
            jax.ShapeDtypeStruct((1, B, N), BF16),
            jax.ShapeDtypeStruct((1, B, N), F32),
            jax.ShapeDtypeStruct((B, D), F32),
        ),
        in_specs=[pl.BlockSpec(memory_space=pl.ANY)] * 3,
        out_specs=[pl.BlockSpec(memory_space=pl.ANY)] * 3,
        scratch_shapes=[vm((2, 2, 8, OWN, L), BF16), vm((32 * OWN, L), F32), vm((B, D), F32), vm((B, N), BF16), vm((B, N), F32), dma((6,))],
        compiler_params=pltpu.CompilerParams(vmem_limit_bytes=60 * 2**20),
    )(*results)


def solution(mesh):
    placed = (
        P("grp", None, "dp"),
        P("grp", None, None),
        P("grp", "fsdp", None),
        P("grp", "fsdp", None),
        P("fsdp", None),
        P("grp", "fsdp", "dp"),
    )
    return jax.shard_map(
        local,
        mesh=mesh,
        in_specs=placed,
        out_specs=(P("grp", "fsdp", "dp"), P("grp", "fsdp", "dp"), P("fsdp", None)),
        check_vma=False,
    )
```

```python
from functools import partial

import jax
import jax.numpy as jnp
from jax import lax
from jax.experimental import pallas as pl
from jax.experimental.pallas import tpu as pltpu
from jax.sharding import PartitionSpec as P

MESH = pl.DeviceIdType.MESH
F32 = jnp.float32
BF16 = jnp.bfloat16
EPSILON = 1e-06
D = 2432
B = 152
H = 608
N = 256
L = 128
E = 2
OWN = 192 // E
GELU_C = 0.7978845608028654
TILES = ((0, 640), (640, 640), (1280, 640), (1920, 512))

C1, C2, B1, B2, G1, G2, O1, O2, N1, N2 = range(10)


def contract_rows(a, b):
    return lax.dot_general(a, b, (((0,), (0,)), ((), ())), preferred_element_type=F32)


def kernel(
    acts_h, mod_h, win_h, wout_h, zw_h, cot_h,
    block_o, grad_o, A16,
    acts, mod, win, wout, zw, cot, in_sem,
    parts, cols, xf, normed, pre, dgelu, hidden, T, stat,
    sC, rC1, mC32, mC16, rC2,
    sB, rB1, mB32, mB16, rB2,
    sN, rN1, mN32, mN16, rN2,
    GG, GO, a2d, rows32, up32,
    carr_s, carr_r, co_s, co_r,
    st_s1, st_r1, st_s2, st_r2,
    cot1_r, zf, F16, zr1, H32, H16, zr2,
    ss, rs, st_ss, st_rs, g_ss, g_rs, c_ss, c_rs, z2_ss, z2_rs, z3_ss, z3_rs, z4_ss, z4_rs,
):
    g = lax.axis_index("grp")
    f = lax.axis_index("fsdp")
    d = lax.axis_index("dp")
    y, x = f // 4, f % 4
    z, c = d // 2, d % 2
    pos = g * 4 + z
    control = g == 0
    base = g == 1

    def at_xy(py, px):
        return (g, py * 4 + px, d)

    def at_z(q):
        return (q // 4, f, (q % 4) * 2 + c)

    sibling = (g, f, z * 2 + (1 - c))
    partner = (1 - g, f, d)

    loads = [
        pltpu.make_async_copy(src, dst, in_sem.at[i])
        for i, (src, dst) in enumerate(
            ((mod_h, mod), (cot_h.at[0], cot), (zw_h, zw), (acts_h.at[0], acts), (win_h.at[0], win), (wout_h.at[0], wout))
        )
    ]
    l_mod, l_cot, l_zw, l_acts, l_win, l_wout = loads
    l_mod.start()
    l_cot.start()

    @pl.when(base)
    def _():
        l_zw.start()

    l_acts.start()
    l_win.start()

    barrier = pltpu.get_barrier_semaphore()
    for k in (1, 2, 3):
        pl.semaphore_signal(barrier, inc=1, device_id=at_xy(y, (x + k) % 4), device_id_type=MESH)
        pl.semaphore_signal(barrier, inc=1, device_id=at_xy((y + k) % 4, x), device_id_type=MESH)
    for k in range(1, 8):
        pl.semaphore_signal(barrier, inc=1, device_id=at_z((pos + k) % 8), device_id_type=MESH)
    pl.semaphore_signal(barrier, inc=1, device_id=sibling, device_id_type=MESH)

    def remote(src, dst, send, recv, where):
        return pltpu.make_async_remote_copy(
            src_ref=src, dst_ref=dst, send_sem=send, recv_sem=recv, device_id=where, device_id_type=MESH
        )

    HK = [(h, k) for k in (1, 3, 2) for h in (0, 1)]

    def peer_x(k):
        return at_xy(y, (x + k) % 4)

    def peer_y(k):
        return at_xy((y + k) % 4, x)

    def rs1(n, s, r1):
        out = []
        for h, k in HK:
            to = (x + k) % 4 if h == 0 else (y + k) % 4
            where = peer_x(k) if h == 0 else peer_y(k)
            out.append(remote(s.at[h, to], r1.at[h, k - 1], ss.at[n, h, k - 1], rs.at[n, h, k - 1], where))
        return out

    def rs2(n, m16, r2):
        out = []
        for h, k in HK:
            to = (y + k) % 4 if h == 0 else (x + k) % 4
            where = peer_y(k) if h == 0 else peer_x(k)
            out.append(remote(m16.at[h, to], r2.at[h, k - 1], ss.at[n, h, k - 1], rs.at[n, h, k - 1], where))
        return out

    def ag1(n, G):
        out = []
        for h, k in HK:
            blk = G.at[0, x, y] if h == 0 else G.at[1, y, x]
            where = peer_y(k) if h == 0 else peer_x(k)
            out.append(remote(blk, blk, ss.at[n, h, k - 1], rs.at[n, h, k - 1], where))
        return out

    def ag2(n, G):
        out = []
        for h, k in HK:
            blk = G.at[0, x] if h == 0 else G.at[1, y]
            where = peer_x(k) if h == 0 else peer_y(k)
            out.append(remote(blk, blk, ss.at[n, h, k - 1], rs.at[n, h, k - 1], where))
        return out

    def ag_block(n, G, h, j):
        if h == 0:
            blk = G.at[0, x, (y + 4 - j) % 4]
            return [remote(blk, blk, ss.at[n, 0, k - 1], rs.at[n, 0, k - 1], peer_x(k)) for k in (1, 3, 2)]
        blk = G.at[1, y, (x + 4 - j) % 4]
        return [remote(blk, blk, ss.at[n, 1, k - 1], rs.at[n, 1, k - 1], peer_y(k)) for k in (1, 3, 2)]

    def ag_start(n, G):
        start(ag1(n, G) + ag_block(n + 1, G, 0, 0) + ag_block(n + 1, G, 1, 0))

    def ag_forward(n, G):
        for (h, j), cp in zip(HK, ag1(n, G)):
            cp.wait_recv()
            start(ag_block(n + 1, G, h, j))

    def start(copies):
        for cp in copies:
            cp.start()

    def arrived(copies):
        for cp in copies:
            cp.wait_recv()

    def sent(copies):
        for cp in copies:
            cp.wait_send()

    def extract(s):
        def body(i, _):
            blk = T[pl.ds(pl.multiple_of(i * B, 8), B), :]
            s[0, i % 4, i // 4] = blk[:, :L].astype(BF16)
            s[1, i // 4, i % 4] = blk[:, L:].astype(BF16)
            return 0

        lax.fori_loop(0, 16, body, 0)

    def rs_mid(s, r1, m32, m16):
        def body(q, _):
            for h in (0, 1):
                own = x if h == 0 else y
                total = s[h, own, q].astype(F32)
                for k in range(3):
                    total = total + r1[h, k, q].astype(F32)
                m32[h, q] = total
                m16[h, q] = total.astype(BF16)
            return 0

        lax.fori_loop(0, 4, body, 0)

    def rs_last(m32, r2, out):
        for h in (0, 1):
            total = m32[h, y if h == 0 else x]
            for k in range(3):
                total = total + r2[h, k].astype(F32)
            out[:, h * L : (h + 1) * L] = total

    def flatten(G):
        def body(i, _):
            yy, xx = i // 2, 2 * (i % 2)
            rows = pl.ds(pl.multiple_of(i * 2 * B, 16), 2 * B)
            for h in (0, 1):
                p, q = (G[0, xx, yy], G[0, xx + 1, yy]) if h == 0 else (G[1, yy, xx], G[1, yy, xx + 1])
                both = jnp.concatenate([p.astype(F32), q.astype(F32)], axis=0)
                a2d[rows, h * L : (h + 1) * L] = both.astype(BF16)
            return 0

        lax.fori_loop(0, 8, body, 0)

    copies_c1, copies_c2 = rs1(C1, sC, rC1), rs2(C2, mC16, rC2)
    copies_b1, copies_b2 = rs1(B1, sB, rB1), rs2(B2, mB16, rB2)
    copies_n1, copies_n2 = rs1(N1, sN, rN1), rs2(N2, mN16, rN2)
    copies_g1, copies_g2 = ag1(G1, GG), ag2(G2, GG)
    copies_o1, copies_o2 = ag1(O1, GO), ag2(O2, GO)
    carr_copy = remote(carr_s, carr_r, g_ss.at[0], g_rs.at[0], partner)
    co_copy = remote(co_s, co_r, g_ss.at[1], g_rs.at[1], partner)
    cot_copy = remote(cot, cot1_r, g_ss.at[2], g_rs.at[2], partner)
    st1 = [remote(st_s1, st_r1.at[k - 1], st_ss.at[0, k - 1], st_rs.at[0, k - 1], peer_x(k)) for k in (1, 2, 3)]
    st2 = [remote(st_s2, st_r2.at[k - 1], st_ss.at[1, k - 1], st_rs.at[1, k - 1], peer_y(k)) for k in (1, 2, 3)]
    z1 = [remote(F16.at[e, 1 - c], zr1.at[e], c_ss.at[e], c_rs.at[e], sibling) for e in range(E)]
    z2 = [
        [
            remote(
                H16.at[e, (pos + k) % 8], zr2.at[e, z], z2_ss.at[e, k - 1], z2_rs.at[e, z], at_z((pos + k) % 8)
            )
            for k in (1, 7, 2, 6, 3, 5, 4)
        ]
        for e in range(E)
    ]

    def z3_copy(e, i, blk, q):
        return remote(blk, blk, z3_ss.at[e, i], z3_rs.at[e, i], at_z(q % 8))

    near = [[z3_copy(e, i, A16.at[e, c, pos], pos + by) for i, by in enumerate((1, 7, 2, 6, 3, 5, 4))] for e in range(E)]
    z4 = [
        [
            remote(
                A16.at[e, c, (pos + k) % 8], A16.at[e, c, (pos + k) % 8], z4_ss.at[e, k], z4_rs.at[e, k], sibling
            )
            for k in range(8)
        ]
        for e in range(E)
    ]

    def z2_arrival(e, zz):
        return remote(H16.at[e, 0], zr2.at[e, zz], z2_ss.at[e, 0], z2_rs.at[e, zz], sibling)

    l_cot.wait()

    @pl.when(base)
    def _():
        l_zw.wait()
        for c0, width in TILES:
            T[c0 : c0 + width, :] = contract_rows(zw[:, c0 : c0 + width], cot[...])
        extract(sC)

    @pl.when(base)
    def _():
        pl.semaphore_wait(barrier, 14)
        start(copies_c1)
        cot_copy.start()

    l_mod.wait()
    row = lax.broadcasted_iota(jnp.int32, (16, L), 0)
    for j in range(D // L):
        at = slice(j * L, (j + 1) * L)
        value = jnp.zeros((16, L), F32)
        for n, m in enumerate((1.0 + mod[1, :, at], mod[0, :, at], mod[2, :, at])):
            high = m.astype(BF16).astype(F32)
            middle = (m - high).astype(BF16).astype(F32)
            for k, part in enumerate((high, middle, (m - high) - middle)):
                value = jnp.where(row == 3 * n + k, part, value)
        parts[:, at] = value.astype(BF16)
    which = lax.broadcasted_iota(jnp.int32, (16, 3 * L), 0) // 3
    column = lax.broadcasted_iota(jnp.int32, (16, 3 * L), 1) // L
    select = jnp.where(which == column, 1.0, 0.0).astype(BF16)
    for c0, width in TILES:
        cols[c0 : c0 + width, :] = contract_rows(parts[:, c0 : c0 + width], select)

    def twice(v):
        return jnp.concatenate([v, v], axis=1)

    def fold(v):
        return jnp.sum(v.reshape(L // 8, 8, N), axis=0)

    l_acts.wait()
    l_wout.start()
    total = jnp.zeros((8, N), F32)
    for j in range(D // L):
        v = acts[j * L : (j + 1) * L, :].astype(F32)
        xf[j * L : (j + 1) * L, :] = v
        total = total + fold(v)
    mean = jnp.sum(total, axis=0, keepdims=True) * (1.0 / D)
    total = jnp.zeros((8, N), F32)
    for j in range(D // L):
        v = xf[j * L : (j + 1) * L, :] - mean
        total = total + fold(v * v)
    variance = jnp.sum(total, axis=0, keepdims=True) * (1.0 / D)
    rstd = lax.rsqrt(variance + EPSILON)
    stat[0:1, :] = mean
    stat[1:2, :] = rstd
    for j in range(D // L):
        at = slice(j * L, (j + 1) * L)
        v = (xf[at, :] - mean) * rstd
        normed[at, :] = (v * twice(cols[at, :L]) + twice(cols[at, L : 2 * L])).astype(BF16)

    l_win.wait()
    half = H // 2
    for i in range(2):
        pre[i * half : (i + 1) * half, :] = jnp.dot(
            win[i * half : (i + 1) * half, :], normed[...], preferred_element_type=F32
        )

    def gelu_body(j, _):
        at = pl.ds(pl.multiple_of(j * 32, 32), 32)
        v = pre[at, :]
        v2 = v * v
        t = jnp.tanh(GELU_C * (v + 0.044715 * (v2 * v)))
        cdf = 0.5 * (1.0 + t)
        hidden[at, :] = (v * cdf).astype(BF16)
        dgelu[at, :] = cdf + 0.5 * v * (1.0 - t * t) * (GELU_C * (1.0 + 3.0 * 0.044715 * v2))
        return 0

    lax.fori_loop(0, H // 32, gelu_body, 0)
    l_wout.wait()

    def produce(n, weights, s, r1, send):
        for yy, (c0, width) in enumerate(TILES):
            T[c0 : c0 + width, :] = contract_rows(weights[:, c0 : c0 + width], hidden[...])
            for xx in range(4):
                blk = T[(yy * 4 + xx) * B : (yy * 4 + xx + 1) * B, :]
                s[0, xx, yy] = blk[:, :L].astype(BF16)
                s[1, yy, xx] = blk[:, L:].astype(BF16)

            @pl.when(send)
            def _():
                for k in (1, 3, 2):
                    to = (x + k) % 4
                    remote(
                        s.at[0, to, yy], r1.at[0, k - 1, yy], ss.at[n, 0, k - 1], rs.at[n, 0, k - 1], peer_x(k)
                    ).start()

            @pl.when(jnp.logical_and(send, y != yy))
            def _():
                k = (yy + 4 - y) % 4
                remote(
                    s.at[1, yy], r1.at[1, k - 1], ss.at[n, 1, k - 1], rs.at[n, 1, k - 1], at_xy(yy, x)
                ).start()

    @pl.when(control)
    def _():
        pl.semaphore_wait(barrier, 14)

    produce(B1, wout, sB, rB1, control)

    own_rows = pl.ds(pl.multiple_of(f * B, 8), B)
    gate_rows = twice(cols[own_rows, 2 * L :])

    def set_gate_grad(up):
        gg = (gate_rows * up).astype(BF16)
        GG[0, x, y] = gg[:, :L]
        GG[1, y, x] = gg[:, L:]

    @pl.when(base)
    def _():
        arrived(copies_c1)
        rs_mid(sC, rC1, mC32, mC16)
        start(copies_c2)
        up = cot[...].astype(F32)
        up32[...] = up
        set_gate_grad(up)
        start(copies_g1)
        arrived(copies_c2)
        rs_last(mC32, rC2, rows32)
        carr_s[...] = rows32[...].astype(BF16)
        carr_copy.start()
        start(copies_b1)
        arrived(copies_g1)
        start(copies_g2)

    arrived(copies_b1)
    rs_mid(sB, rB1, mB32, mB16)
    start(copies_b2)
    arrived(copies_b2)
    rs_last(mB32, rB2, rows32)
    rows32[...] = xf[own_rows, :] + gate_rows * rows32[...]

    @pl.when(control)
    def _():
        out = rows32[...].astype(BF16)
        block_o[...] = out
        co_s[...] = out
        co_copy.start()
        GO[0, x, y] = out[:, :L]
        GO[1, y, x] = out[:, L:]
        ag_start(O1, GO)
        carr_copy.wait_recv()
        up = carr_r[...].astype(F32) + cot[...].astype(F32)
        up32[...] = up
        set_gate_grad(up)
        start(copies_g1)
        ag_forward(O1, GO)
        cot_copy.wait_recv()
        zf[19 * B :, :] = jnp.zeros((16 * E * OWN - 19 * B, L), F32)

        arrived(copies_o2)
        arrived(copies_g1)
        start(copies_g2)
        flatten(GO)
        for c0, width in TILES:
            term = lax.dot_general(
                cot1_r[...], a2d[c0 : c0 + width, :], (((1,), (1,)), ((), ())), preferred_element_type=F32
            )
            for t in range(width // L):
                r0 = (c0 // L + t) * B
                zf[r0 : r0 + B, :] = term[:, t * L : (t + 1) * L]

        for e in range(E):

            def flat_body(o, _):
                at = pl.ds(pl.multiple_of((e * 16 + o) * OWN, OWN), OWN)
                F16[e, o // 8, o % 8] = zf[at, :].astype(BF16)
                return 0

            lax.fori_loop(0, 16, flat_body, 0)
            z1[e].start()

    @pl.when(base)
    def _():
        co_copy.wait_recv()
        GO[0, x, y] = co_r[:, :L]
        GO[1, y, x] = co_r[:, L:]
        start(copies_o1)

    @pl.when(control)
    def _():
        for e in range(E):
            z1[e].wait_recv()

            def pair_body(q, _):
                at = pl.ds(pl.multiple_of((e * 16 + c * 8 + q) * OWN, OWN), OWN)
                total = zf[at, :] + zr1[e, q].astype(F32)
                H32[e, q] = total
                H16[e, q] = total.astype(BF16)
                return 0

            lax.fori_loop(0, 8, pair_body, 0)
            start(z2[e])

    arrived(copies_g2)
    flatten(GG)
    for i in range(2):
        hg = jnp.dot(wout[i * half : (i + 1) * half, :], a2d[...], preferred_element_type=F32)
        hidden[i * half : (i + 1) * half, :] = (hg * dgelu[i * half : (i + 1) * half, :]).astype(BF16)

    @pl.when(base)
    def _():
        arrived(copies_o1)
        start(copies_o2)

    produce(N1, win, sN, rN1, g >= 0)
    p1 = jnp.zeros((8, N), F32)
    p2 = jnp.zeros((8, N), F32)
    for j in range(D // L):
        at = slice(j * L, (j + 1) * L)
        v = T[at, :] * twice(cols[at, :L])
        p1 = p1 + fold(v)
        p2 = p2 + fold(v * ((xf[at, :] - stat[0:1, :]) * stat[1:2, :]))
    st_s1[0:8, :] = p1
    st_s1[8:16, :] = p2
    start(st1)

    for e in range(E):

        @pl.when(control)
        def _():
            for k in (1, 2, 3):
                z2_arrival(e, (z + k) % 4).wait_recv()
            total = H32[e, pos]
            for k in (1, 2, 3):
                total = total + zr2[e, (z + k) % 4].astype(F32)
            A16[e, c, pos] = total.astype(BF16)

        @pl.when(base)
        def _():
            for k in range(4):
                z2_arrival(e, k).wait_recv()
            total = zr2[e, 0].astype(F32)
            for k in (1, 2, 3):
                total = total + zr2[e, k].astype(F32)
            A16[e, c, pos] = total.astype(BF16)

        start(near[e])
        z4[e][0].start()

    arrived(copies_n1)
    rs_mid(sN, rN1, mN32, mN16)
    start(copies_n2)
    arrived(st1)
    st_s2[...] = st_s1[...] + st_r1[0] + st_r1[1] + st_r1[2]
    start(st2)

    @pl.when(base)
    def _():
        arrived(copies_o2)
        flatten(GO)
        residual = jnp.dot(zw[...], a2d[...], preferred_element_type=F32)
        block_o[...] = (rows32[...] + residual).astype(BF16)

    for e in range(E):
        arrived(near[e])
        start(z4[e][1:])

    arrived(copies_n2)
    arrived(st2)
    rs_last(mN32, rN2, rows32)
    both = st_s2[...] + st_r2[0] + st_r2[1] + st_r2[2]
    m1 = jnp.sum(both[0:8, :], axis=0, keepdims=True) * (1.0 / D)
    m2 = jnp.sum(both[8:16, :], axis=0, keepdims=True) * (1.0 / D)
    xhat = (xf[own_rows, :] - stat[0:1, :]) * stat[1:2, :]
    ghat = rows32[...] * twice(cols[own_rows, :L])
    grad_o[...] = up32[...] + stat[1:2, :] * (ghat - m1 - xhat * m2)

    for e in range(E):
        arrived(z4[e])

    sent(copies_b1 + copies_b2 + copies_g1 + copies_g2 + copies_o1 + copies_o2 + copies_n1 + copies_n2)
    sent(st1 + st2)
    for e in range(E):
        sent(near[e] + z4[e])

    @pl.when(base)
    def _():
        sent(copies_c1 + copies_c2 + [carr_copy, cot_copy])

    @pl.when(control)
    def _():
        sent(z1 + [co_copy])
        for e in range(E):
            sent(z2[e])


def finish(block, grad, flat, block_o, grad_o, zero_o, flat_v, zf, rows, block_v, grad_v, sem):
    def move(src, dst, i):
        cp = pltpu.make_async_copy(src, dst, sem.at[i])
        cp.start()
        return cp

    ins = [move(flat, flat_v, 0), move(grad, grad_v, 1), move(block, block_v, 2)]
    ins[1].wait()
    outs = [move(grad_v, grad_o.at[0], 3)]
    ins[2].wait()
    outs.append(move(block_v, block_o.at[0], 4))
    ins[0].wait()
    for o in range(16 * E):
        zf[o * OWN : (o + 1) * OWN, :] = flat_v[o // 16, (o // 8) % 2, o % 8].astype(F32)
    for t in range(19):
        rows[:, t * L : (t + 1) * L] = zf[t * B : (t + 1) * B, :]
    outs.append(move(rows, zero_o, 5))
    for cp in outs:
        cp.wait()


def local(acts, modulation, w_in, w_out, zero_weight, cotangent):
    vm = pltpu.VMEM
    dma = pltpu.SemaphoreType.DMA

    def rs_bufs():
        return [vm((2, 4, 4, B, L), BF16), vm((2, 3, 4, B, L), BF16), vm((2, 4, B, L), F32), vm((2, 4, B, L), BF16), vm((2, 3, B, L), BF16)]

    scratch = [
        vm((D, N), BF16), vm((3, 1, D), F32), vm((H, D), BF16), vm((H, D), BF16), vm((B, D), BF16), vm((B, N), BF16), dma((6,)),
        vm((16, D), BF16), vm((D, 3 * L), F32), vm((D, N), F32), vm((D, N), BF16), vm((H, N), F32), vm((H, N), F32), vm((H, N), BF16), vm((D, N), F32), vm((8, N), F32),
        *rs_bufs(), *rs_bufs(), *rs_bufs(),
        vm((2, 4, 4, B, L), BF16), vm((2, 4, 4, B, L), BF16), vm((D, N), BF16), vm((B, N), F32), vm((B, N), F32),
        vm((B, N), BF16), vm((B, N), BF16), vm((B, N), BF16), vm((B, N), BF16),
        vm((16, N), F32), vm((3, 16, N), F32), vm((16, N), F32), vm((3, 16, N), F32),
        vm((B, N), BF16), vm((16 * E * OWN, L), F32), vm((E, 2, 8, OWN, L), BF16), vm((E, 8, OWN, L), BF16),
        vm((E, 8, OWN, L), F32), vm((E, 8, OWN, L), BF16), vm((E, 4, OWN, L), BF16),
        dma((10, 2, 3)), dma((10, 2, 3)), dma((2, 3)), dma((2, 3)), dma((3,)), dma((3,)), dma((E,)), dma((E,)),
        dma((E, 7)), dma((E, 4)), dma((E, 7)), dma((E, 7)), dma((E, 8)), dma((E, 8)),
    ]
    results = pl.pallas_call(
        kernel,
        out_shape=(
            jax.ShapeDtypeStruct((B, N), BF16),
            jax.ShapeDtypeStruct((B, N), F32),
            jax.ShapeDtypeStruct((E, 2, 8, OWN, L), BF16),
        ),
        in_specs=[pl.BlockSpec(memory_space=pl.ANY)] * 6,
        out_specs=[pl.BlockSpec(memory_space=pltpu.VMEM)] * 3,
        scratch_shapes=scratch,
        compiler_params=pltpu.CompilerParams(
            collective_id=0, has_side_effects=True, vmem_limit_bytes=60 * 2**20
        ),
    )(acts, jnp.transpose(modulation, (1, 0, 2)), w_in, w_out, zero_weight, cotangent)
    return pl.pallas_call(
        finish,
        out_shape=(
            jax.ShapeDtypeStruct((1, B, N), BF16),
            jax.ShapeDtypeStruct((1, B, N), F32),
            jax.ShapeDtypeStruct((B, D), F32),
        ),
        in_specs=[pl.BlockSpec(memory_space=pl.ANY)] * 3,
        out_specs=[pl.BlockSpec(memory_space=pl.ANY)] * 3,
        scratch_shapes=[vm((E, 2, 8, OWN, L), BF16), vm((16 * E * OWN, L), F32), vm((B, D), F32), vm((B, N), BF16), vm((B, N), F32), dma((6,))],
        compiler_params=pltpu.CompilerParams(vmem_limit_bytes=60 * 2**20),
    )(*results)


def solution(mesh):
    placed = (
        P("grp", None, "dp"),
        P("grp", None, None),
        P("grp", "fsdp", None),
        P("grp", "fsdp", None),
        P("fsdp", None),
        P("grp", "fsdp", "dp"),
    )
    return jax.shard_map(
        local,
        mesh=mesh,
        in_specs=placed,
        out_specs=(P("grp", "fsdp", "dp"), P("grp", "fsdp", "dp"), P("fsdp", None)),
        check_vma=False,
    )
```

```python
from functools import partial

import jax
import jax.numpy as jnp
from jax import lax
from jax.experimental import pallas as pl
from jax.experimental.pallas import tpu as pltpu
from jax.sharding import PartitionSpec as P

MESH = pl.DeviceIdType.MESH
F32 = jnp.float32
BF16 = jnp.bfloat16
EPSILON = 1e-06
D = 2432
B = 152
H = 608
N = 256
L = 128
E = 2
OWN = 192 // E
GELU_C = 0.7978845608028654
TILES = ((0, 640), (640, 640), (1280, 640), (1920, 512))

C1, C2, B1, B2, G1, G2, O1, O2, N1, N2 = range(10)


def contract_rows(a, b):
    return lax.dot_general(a, b, (((0,), (0,)), ((), ())), preferred_element_type=F32)


def kernel(
    acts_h, mod_h, win_h, wout_h, zw_h, cot_h,
    block_o, grad_o, A16,
    acts, mod, win, wout, zw, cot, in_sem,
    parts, cols, xf, normed, pre, dgelu, hidden, T, stat,
    sC, rC1, mC32, mC16, rC2,
    sB, rB1, mB32, mB16, rB2,
    sN, rN1, mN32, mN16, rN2,
    GG, GO, a2d, rows32, up32,
    carr_s, carr_r, co_s, co_r,
    st_s1, st_r1, st_s2, st_r2,
    cot1_r, zf, F16, zr1, H32, H16, zr2,
    ss, rs, st_ss, st_rs, g_ss, g_rs, c_ss, c_rs, z2_ss, z2_rs, z3_ss, z3_rs, z4_ss, z4_rs,
):
    g = lax.axis_index("grp")
    f = lax.axis_index("fsdp")
    d = lax.axis_index("dp")
    y, x = f // 4, f % 4
    z, c = d // 2, d % 2
    pos = g * 4 + z
    control = g == 0
    base = g == 1

    def at_xy(py, px):
        return (g, py * 4 + px, d)

    def at_z(q):
        return (q // 4, f, (q % 4) * 2 + c)

    sibling = (g, f, z * 2 + (1 - c))
    partner = (1 - g, f, d)

    loads = [
        pltpu.make_async_copy(src, dst, in_sem.at[i])
        for i, (src, dst) in enumerate(
            ((mod_h, mod), (cot_h.at[0], cot), (zw_h, zw), (acts_h.at[0], acts), (win_h.at[0], win), (wout_h.at[0], wout))
        )
    ]
    l_mod, l_cot, l_zw, l_acts, l_win, l_wout = loads
    l_mod.start()
    l_cot.start()

    @pl.when(base)
    def _():
        l_zw.start()

    l_acts.start()
    l_win.start()

    barrier = pltpu.get_barrier_semaphore()
    for k in (1, 2, 3):
        pl.semaphore_signal(barrier, inc=1, device_id=at_xy(y, (x + k) % 4), device_id_type=MESH)
        pl.semaphore_signal(barrier, inc=1, device_id=at_xy((y + k) % 4, x), device_id_type=MESH)
    for k in range(1, 8):
        pl.semaphore_signal(barrier, inc=1, device_id=at_z((pos + k) % 8), device_id_type=MESH)
    pl.semaphore_signal(barrier, inc=1, device_id=sibling, device_id_type=MESH)

    def remote(src, dst, send, recv, where):
        return pltpu.make_async_remote_copy(
            src_ref=src, dst_ref=dst, send_sem=send, recv_sem=recv, device_id=where, device_id_type=MESH
        )

    HK = [(h, k) for k in (1, 3, 2) for h in (0, 1)]

    def peer_x(k):
        return at_xy(y, (x + k) % 4)

    def peer_y(k):
        return at_xy((y + k) % 4, x)

    def rs1(n, s, r1):
        out = []
        for h, k in HK:
            to = (x + k) % 4 if h == 0 else (y + k) % 4
            where = peer_x(k) if h == 0 else peer_y(k)
            out.append(remote(s.at[h, to], r1.at[h, k - 1], ss.at[n, h, k - 1], rs.at[n, h, k - 1], where))
        return out

    def rs2(n, m16, r2):
        out = []
        for h, k in HK:
            to = (y + k) % 4 if h == 0 else (x + k) % 4
            where = peer_y(k) if h == 0 else peer_x(k)
            out.append(remote(m16.at[h, to], r2.at[h, k - 1], ss.at[n, h, k - 1], rs.at[n, h, k - 1], where))
        return out

    def ag1(n, G):
        out = []
        for h, k in HK:
            blk = G.at[0, x, y] if h == 0 else G.at[1, y, x]
            where = peer_y(k) if h == 0 else peer_x(k)
            out.append(remote(blk, blk, ss.at[n, h, k - 1], rs.at[n, h, k - 1], where))
        return out

    def ag2(n, G):
        out = []
        for h, k in HK:
            blk = G.at[0, x] if h == 0 else G.at[1, y]
            where = peer_x(k) if h == 0 else peer_y(k)
            out.append(remote(blk, blk, ss.at[n, h, k - 1], rs.at[n, h, k - 1], where))
        return out

    def ag_block(n, G, h, j):
        if h == 0:
            blk = G.at[0, x, (y + 4 - j) % 4]
            return [remote(blk, blk, ss.at[n, 0, k - 1], rs.at[n, 0, k - 1], peer_x(k)) for k in (1, 3, 2)]
        blk = G.at[1, y, (x + 4 - j) % 4]
        return [remote(blk, blk, ss.at[n, 1, k - 1], rs.at[n, 1, k - 1], peer_y(k)) for k in (1, 3, 2)]

    def ag_start(n, G):
        start(ag1(n, G) + ag_block(n + 1, G, 0, 0) + ag_block(n + 1, G, 1, 0))

    def ag_forward(n, G):
        for (h, j), cp in zip(HK, ag1(n, G)):
            cp.wait_recv()
            start(ag_block(n + 1, G, h, j))

    def start(copies):
        for cp in copies:
            cp.start()

    def arrived(copies):
        for cp in copies:
            cp.wait_recv()

    def sent(copies):
        for cp in copies:
            cp.wait_send()

    def extract(s):
        def body(i, _):
            blk = T[pl.ds(pl.multiple_of(i * B, 8), B), :]
            s[0, i % 4, i // 4] = blk[:, :L].astype(BF16)
            s[1, i // 4, i % 4] = blk[:, L:].astype(BF16)
            return 0

        lax.fori_loop(0, 16, body, 0)

    def rs_mid(s, r1, m32, m16):
        def body(q, _):
            for h in (0, 1):
                own = x if h == 0 else y
                total = s[h, own, q].astype(F32)
                for k in range(3):
                    total = total + r1[h, k, q].astype(F32)
                m32[h, q] = total
                m16[h, q] = total.astype(BF16)
            return 0

        lax.fori_loop(0, 4, body, 0)

    def rs_last(m32, r2, out):
        for h in (0, 1):
            total = m32[h, y if h == 0 else x]
            for k in range(3):
                total = total + r2[h, k].astype(F32)
            out[:, h * L : (h + 1) * L] = total

    def flatten(G):
        def body(i, _):
            yy, xx = i // 2, 2 * (i % 2)
            rows = pl.ds(pl.multiple_of(i * 2 * B, 16), 2 * B)
            for h in (0, 1):
                p, q = (G[0, xx, yy], G[0, xx + 1, yy]) if h == 0 else (G[1, yy, xx], G[1, yy, xx + 1])
                both = jnp.concatenate([p.astype(F32), q.astype(F32)], axis=0)
                a2d[rows, h * L : (h + 1) * L] = both.astype(BF16)
            return 0

        lax.fori_loop(0, 8, body, 0)

    copies_c1, copies_c2 = rs1(C1, sC, rC1), rs2(C2, mC16, rC2)
    copies_b1, copies_b2 = rs1(B1, sB, rB1), rs2(B2, mB16, rB2)
    copies_n1, copies_n2 = rs1(N1, sN, rN1), rs2(N2, mN16, rN2)
    copies_g1, copies_g2 = ag1(G1, GG), ag2(G2, GG)
    copies_o1, copies_o2 = ag1(O1, GO), ag2(O2, GO)
    carr_copy = remote(carr_s, carr_r, g_ss.at[0], g_rs.at[0], partner)
    co_copy = remote(co_s, co_r, g_ss.at[1], g_rs.at[1], partner)
    cot_copy = remote(cot, cot1_r, g_ss.at[2], g_rs.at[2], partner)
    st1 = [remote(st_s1, st_r1.at[k - 1], st_ss.at[0, k - 1], st_rs.at[0, k - 1], peer_x(k)) for k in (1, 2, 3)]
    st2 = [remote(st_s2, st_r2.at[k - 1], st_ss.at[1, k - 1], st_rs.at[1, k - 1], peer_y(k)) for k in (1, 2, 3)]
    z1 = [remote(F16.at[e, 1 - c], zr1.at[e], c_ss.at[e], c_rs.at[e], sibling) for e in range(E)]
    z2 = [
        [
            remote(
                H16.at[e, (pos + k) % 8], zr2.at[e, z], z2_ss.at[e, k - 1], z2_rs.at[e, z], at_z((pos + k) % 8)
            )
            for k in (1, 7, 2, 6, 3, 5, 4)
        ]
        for e in range(E)
    ]

    def z3_copy(e, i, blk, q):
        return remote(blk, blk, z3_ss.at[e, i], z3_rs.at[e, i], at_z(q % 8))

    near = [[z3_copy(e, i, A16.at[e, c, pos], pos + by) for i, by in enumerate((1, 7, 2, 6, 3, 5, 4))] for e in range(E)]
    z4 = [
        [
            remote(
                A16.at[e, c, (pos + k) % 8], A16.at[e, c, (pos + k) % 8], z4_ss.at[e, k], z4_rs.at[e, k], sibling
            )
            for k in range(8)
        ]
        for e in range(E)
    ]

    def z2_arrival(e, zz):
        return remote(H16.at[e, 0], zr2.at[e, zz], z2_ss.at[e, 0], z2_rs.at[e, zz], sibling)

    l_cot.wait()

    @pl.when(base)
    def _():
        l_zw.wait()
        for c0, width in TILES:
            T[c0 : c0 + width, :] = contract_rows(zw[:, c0 : c0 + width], cot[...])
        extract(sC)

    @pl.when(base)
    def _():
        pl.semaphore_wait(barrier, 14)
        start(copies_c1)
        cot_copy.start()

    l_mod.wait()
    row = lax.broadcasted_iota(jnp.int32, (16, L), 0)
    for j in range(D // L):
        at = slice(j * L, (j + 1) * L)
        value = jnp.zeros((16, L), F32)
        for n, m in enumerate((1.0 + mod[1, :, at], mod[0, :, at], mod[2, :, at])):
            high = m.astype(BF16).astype(F32)
            middle = (m - high).astype(BF16).astype(F32)
            for k, part in enumerate((high, middle, (m - high) - middle)):
                value = jnp.where(row == 3 * n + k, part, value)
        parts[:, at] = value.astype(BF16)
    which = lax.broadcasted_iota(jnp.int32, (16, 3 * L), 0) // 3
    column = lax.broadcasted_iota(jnp.int32, (16, 3 * L), 1) // L
    select = jnp.where(which == column, 1.0, 0.0).astype(BF16)
    for c0, width in TILES:
        cols[c0 : c0 + width, :] = contract_rows(parts[:, c0 : c0 + width], select)

    def twice(v):
        return jnp.concatenate([v, v], axis=1)

    def fold(v):
        return jnp.sum(v.reshape(L // 8, 8, N), axis=0)

    l_acts.wait()
    l_wout.start()
    total = jnp.zeros((8, N), F32)
    for j in range(D // L):
        v = acts[j * L : (j + 1) * L, :].astype(F32)
        xf[j * L : (j + 1) * L, :] = v
        total = total + fold(v)
    mean = jnp.sum(total, axis=0, keepdims=True) * (1.0 / D)
    total = jnp.zeros((8, N), F32)
    for j in range(D // L):
        v = xf[j * L : (j + 1) * L, :] - mean
        total = total + fold(v * v)
    variance = jnp.sum(total, axis=0, keepdims=True) * (1.0 / D)
    rstd = lax.rsqrt(variance + EPSILON)
    stat[0:1, :] = mean
    stat[1:2, :] = rstd
    for j in range(D // L):
        at = slice(j * L, (j + 1) * L)
        v = (xf[at, :] - mean) * rstd
        normed[at, :] = (v * twice(cols[at, :L]) + twice(cols[at, L : 2 * L])).astype(BF16)

    l_win.wait()
    half = H // 2
    for i in range(2):
        pre[i * half : (i + 1) * half, :] = jnp.dot(
            win[i * half : (i + 1) * half, :], normed[...], preferred_element_type=F32
        )

    def gelu_body(j, _):
        at = pl.ds(pl.multiple_of(j * 32, 32), 32)
        v = pre[at, :]
        v2 = v * v
        t = jnp.tanh(GELU_C * (v + 0.044715 * (v2 * v)))
        cdf = 0.5 * (1.0 + t)
        hidden[at, :] = (v * cdf).astype(BF16)
        dgelu[at, :] = cdf + 0.5 * v * (1.0 - t * t) * (GELU_C * (1.0 + 3.0 * 0.044715 * v2))
        return 0

    lax.fori_loop(0, H // 32, gelu_body, 0)
    l_wout.wait()

    def produce(n, weights, s, r1, send):
        for yy, (c0, width) in enumerate(TILES):
            T[c0 : c0 + width, :] = contract_rows(weights[:, c0 : c0 + width], hidden[...])
            for xx in range(4):
                blk = T[(yy * 4 + xx) * B : (yy * 4 + xx + 1) * B, :]
                s[0, xx, yy] = blk[:, :L].astype(BF16)
                s[1, yy, xx] = blk[:, L:].astype(BF16)

            @pl.when(send)
            def _():
                for k in (1, 3, 2):
                    to = (x + k) % 4
                    remote(
                        s.at[0, to, yy], r1.at[0, k - 1, yy], ss.at[n, 0, k - 1], rs.at[n, 0, k - 1], peer_x(k)
                    ).start()

            @pl.when(jnp.logical_and(send, y != yy))
            def _():
                k = (yy + 4 - y) % 4
                remote(
                    s.at[1, yy], r1.at[1, k - 1], ss.at[n, 1, k - 1], rs.at[n, 1, k - 1], at_xy(yy, x)
                ).start()

    @pl.when(control)
    def _():
        pl.semaphore_wait(barrier, 14)

    produce(B1, wout, sB, rB1, control)

    own_rows = pl.ds(pl.multiple_of(f * B, 8), B)
    gate_rows = twice(cols[own_rows, 2 * L :])

    def set_gate_grad(up):
        gg = (gate_rows * up).astype(BF16)
        GG[0, x, y] = gg[:, :L]
        GG[1, y, x] = gg[:, L:]

    @pl.when(base)
    def _():
        arrived(copies_c1)
        rs_mid(sC, rC1, mC32, mC16)
        start(copies_c2)
        up = cot[...].astype(F32)
        up32[...] = up
        set_gate_grad(up)
        start(copies_g1)
        arrived(copies_c2)
        rs_last(mC32, rC2, rows32)
        carr_s[...] = rows32[...].astype(BF16)
        carr_copy.start()
        start(copies_b1)
        arrived(copies_g1)
        start(copies_g2)

    def branch_mid():
        arrived(copies_b1)
        rs_mid(sB, rB1, mB32, mB16)
        start(copies_b2)

    def branch_rows():
        arrived(copies_b2)
        rs_last(mB32, rB2, rows32)
        rows32[...] = xf[own_rows, :] + gate_rows * rows32[...]

    @pl.when(control)
    def _():
        branch_mid()
        branch_rows()
        out = rows32[...].astype(BF16)
        block_o[...] = out
        co_s[...] = out
        co_copy.start()
        GO[0, x, y] = out[:, :L]
        GO[1, y, x] = out[:, L:]
        ag_start(O1, GO)
        carr_copy.wait_recv()
        up = carr_r[...].astype(F32) + cot[...].astype(F32)
        up32[...] = up
        set_gate_grad(up)
        start(copies_g1)
        ag_forward(O1, GO)
        cot_copy.wait_recv()
        zf[19 * B :, :] = jnp.zeros((16 * E * OWN - 19 * B, L), F32)

        arrived(copies_o2)
        arrived(copies_g1)
        start(copies_g2)
        flatten(GO)
        for c0, width in TILES:
            term = lax.dot_general(
                cot1_r[...], a2d[c0 : c0 + width, :], (((1,), (1,)), ((), ())), preferred_element_type=F32
            )
            for t in range(width // L):
                r0 = (c0 // L + t) * B
                zf[r0 : r0 + B, :] = term[:, t * L : (t + 1) * L]

        for e in range(E):

            def flat_body(o, _):
                at = pl.ds(pl.multiple_of((e * 16 + o) * OWN, OWN), OWN)
                F16[e, o // 8, o % 8] = zf[at, :].astype(BF16)
                return 0

            lax.fori_loop(0, 16, flat_body, 0)
            z1[e].start()

    @pl.when(base)
    def _():
        co_copy.wait_recv()
        GO[0, x, y] = co_r[:, :L]
        GO[1, y, x] = co_r[:, L:]
        start(copies_o1)

    @pl.when(control)
    def _():
        for e in range(E):
            z1[e].wait_recv()

            def pair_body(q, _):
                at = pl.ds(pl.multiple_of((e * 16 + c * 8 + q) * OWN, OWN), OWN)
                total = zf[at, :] + zr1[e, q].astype(F32)
                H32[e, q] = total
                H16[e, q] = total.astype(BF16)
                return 0

            lax.fori_loop(0, 8, pair_body, 0)
            start(z2[e])

    arrived(copies_g2)
    flatten(GG)
    for i in range(2):
        hg = jnp.dot(wout[i * half : (i + 1) * half, :], a2d[...], preferred_element_type=F32)
        hidden[i * half : (i + 1) * half, :] = (hg * dgelu[i * half : (i + 1) * half, :]).astype(BF16)

    @pl.when(base)
    def _():
        arrived(copies_o1)
        start(copies_o2)

    produce(N1, win, sN, rN1, g >= 0)
    p1 = jnp.zeros((8, N), F32)
    p2 = jnp.zeros((8, N), F32)
    for j in range(D // L):
        at = slice(j * L, (j + 1) * L)
        v = T[at, :] * twice(cols[at, :L])
        p1 = p1 + fold(v)
        p2 = p2 + fold(v * ((xf[at, :] - stat[0:1, :]) * stat[1:2, :]))
    st_s1[0:8, :] = p1
    st_s1[8:16, :] = p2
    start(st1)

    @pl.when(base)
    def _():
        branch_mid()

    for e in range(E):

        @pl.when(control)
        def _():
            for k in (1, 2, 3):
                z2_arrival(e, (z + k) % 4).wait_recv()
            total = H32[e, pos]
            for k in (1, 2, 3):
                total = total + zr2[e, (z + k) % 4].astype(F32)
            A16[e, c, pos] = total.astype(BF16)

        @pl.when(base)
        def _():
            for k in range(4):
                z2_arrival(e, k).wait_recv()
            total = zr2[e, 0].astype(F32)
            for k in (1, 2, 3):
                total = total + zr2[e, k].astype(F32)
            A16[e, c, pos] = total.astype(BF16)

        start(near[e])
        z4[e][0].start()

    arrived(copies_n1)
    rs_mid(sN, rN1, mN32, mN16)
    start(copies_n2)
    arrived(st1)
    st_s2[...] = st_s1[...] + st_r1[0] + st_r1[1] + st_r1[2]
    start(st2)

    @pl.when(base)
    def _():
        branch_rows()
        arrived(copies_o2)
        flatten(GO)
        residual = jnp.dot(zw[...], a2d[...], preferred_element_type=F32)
        block_o[...] = (rows32[...] + residual).astype(BF16)

    for e in range(E):
        for cp, k in zip(near[e], (7, 1, 6, 2, 5, 3, 4)):
            cp.wait_recv()
            z4[e][k].start()

    arrived(copies_n2)
    arrived(st2)
    rs_last(mN32, rN2, rows32)
    both = st_s2[...] + st_r2[0] + st_r2[1] + st_r2[2]
    m1 = jnp.sum(both[0:8, :], axis=0, keepdims=True) * (1.0 / D)
    m2 = jnp.sum(both[8:16, :], axis=0, keepdims=True) * (1.0 / D)
    xhat = (xf[own_rows, :] - stat[0:1, :]) * stat[1:2, :]
    ghat = rows32[...] * twice(cols[own_rows, :L])
    grad_o[...] = up32[...] + stat[1:2, :] * (ghat - m1 - xhat * m2)

    for e in range(E):
        arrived(z4[e])

    sent(copies_b1 + copies_b2 + copies_g1 + copies_g2 + copies_o1 + copies_o2 + copies_n1 + copies_n2)
    sent(st1 + st2)
    for e in range(E):
        sent(near[e] + z4[e])

    @pl.when(base)
    def _():
        sent(copies_c1 + copies_c2 + [carr_copy, cot_copy])

    @pl.when(control)
    def _():
        sent(z1 + [co_copy])
        for e in range(E):
            sent(z2[e])


def finish(block, grad, flat, block_o, grad_o, zero_o, flat_v, zf, rows, block_v, grad_v, sem):
    def move(src, dst, i):
        cp = pltpu.make_async_copy(src, dst, sem.at[i])
        cp.start()
        return cp

    ins = [move(flat, flat_v, 0), move(grad, grad_v, 1), move(block, block_v, 2)]
    ins[1].wait()
    outs = [move(grad_v, grad_o.at[0], 3)]
    ins[2].wait()
    outs.append(move(block_v, block_o.at[0], 4))
    ins[0].wait()
    for o in range(16 * E):
        zf[o * OWN : (o + 1) * OWN, :] = flat_v[o // 16, (o // 8) % 2, o % 8].astype(F32)
    for t in range(19):
        rows[:, t * L : (t + 1) * L] = zf[t * B : (t + 1) * B, :]
    outs.append(move(rows, zero_o, 5))
    for cp in outs:
        cp.wait()


def local(acts, modulation, w_in, w_out, zero_weight, cotangent):
    vm = pltpu.VMEM
    dma = pltpu.SemaphoreType.DMA

    def rs_bufs():
        return [vm((2, 4, 4, B, L), BF16), vm((2, 3, 4, B, L), BF16), vm((2, 4, B, L), F32), vm((2, 4, B, L), BF16), vm((2, 3, B, L), BF16)]

    scratch = [
        vm((D, N), BF16), vm((3, 1, D), F32), vm((H, D), BF16), vm((H, D), BF16), vm((B, D), BF16), vm((B, N), BF16), dma((6,)),
        vm((16, D), BF16), vm((D, 3 * L), F32), vm((D, N), F32), vm((D, N), BF16), vm((H, N), F32), vm((H, N), F32), vm((H, N), BF16), vm((D, N), F32), vm((8, N), F32),
        *rs_bufs(), *rs_bufs(), *rs_bufs(),
        vm((2, 4, 4, B, L), BF16), vm((2, 4, 4, B, L), BF16), vm((D, N), BF16), vm((B, N), F32), vm((B, N), F32),
        vm((B, N), BF16), vm((B, N), BF16), vm((B, N), BF16), vm((B, N), BF16),
        vm((16, N), F32), vm((3, 16, N), F32), vm((16, N), F32), vm((3, 16, N), F32),
        vm((B, N), BF16), vm((16 * E * OWN, L), F32), vm((E, 2, 8, OWN, L), BF16), vm((E, 8, OWN, L), BF16),
        vm((E, 8, OWN, L), F32), vm((E, 8, OWN, L), BF16), vm((E, 4, OWN, L), BF16),
        dma((10, 2, 3)), dma((10, 2, 3)), dma((2, 3)), dma((2, 3)), dma((3,)), dma((3,)), dma((E,)), dma((E,)),
        dma((E, 7)), dma((E, 4)), dma((E, 7)), dma((E, 7)), dma((E, 8)), dma((E, 8)),
    ]
    results = pl.pallas_call(
        kernel,
        out_shape=(
            jax.ShapeDtypeStruct((B, N), BF16),
            jax.ShapeDtypeStruct((B, N), F32),
            jax.ShapeDtypeStruct((E, 2, 8, OWN, L), BF16),
        ),
        in_specs=[pl.BlockSpec(memory_space=pl.ANY)] * 6,
        out_specs=[pl.BlockSpec(memory_space=pltpu.VMEM)] * 3,
        scratch_shapes=scratch,
        compiler_params=pltpu.CompilerParams(
            collective_id=0, has_side_effects=True, vmem_limit_bytes=60 * 2**20
        ),
    )(acts, jnp.transpose(modulation, (1, 0, 2)), w_in, w_out, zero_weight, cotangent)
    return pl.pallas_call(
        finish,
        out_shape=(
            jax.ShapeDtypeStruct((1, B, N), BF16),
            jax.ShapeDtypeStruct((1, B, N), F32),
            jax.ShapeDtypeStruct((B, D), F32),
        ),
        in_specs=[pl.BlockSpec(memory_space=pl.ANY)] * 3,
        out_specs=[pl.BlockSpec(memory_space=pl.ANY)] * 3,
        scratch_shapes=[vm((E, 2, 8, OWN, L), BF16), vm((16 * E * OWN, L), F32), vm((B, D), F32), vm((B, N), BF16), vm((B, N), F32), dma((6,))],
        compiler_params=pltpu.CompilerParams(vmem_limit_bytes=60 * 2**20),
    )(*results)


def solution(mesh):
    placed = (
        P("grp", None, "dp"),
        P("grp", None, None),
        P("grp", "fsdp", None),
        P("grp", "fsdp", None),
        P("fsdp", None),
        P("grp", "fsdp", "dp"),
    )
    return jax.shard_map(
        local,
        mesh=mesh,
        in_specs=placed,
        out_specs=(P("grp", "fsdp", "dp"), P("grp", "fsdp", "dp"), P("fsdp", None)),
        check_vma=False,
    )
```

```python
from functools import partial

import jax
import jax.numpy as jnp
from jax import lax
from jax.experimental import pallas as pl
from jax.experimental.pallas import tpu as pltpu
from jax.sharding import PartitionSpec as P

MESH = pl.DeviceIdType.MESH
F32 = jnp.float32
BF16 = jnp.bfloat16
EPSILON = 1e-06
D = 2432
B = 152
H = 608
N = 256
L = 128
E = 2
OWN = 192 // E
GELU_C = 0.7978845608028654
TILES = ((0, 640), (640, 640), (1280, 640), (1920, 512))

C1, C2, B1, B2, G1, G2, O1, O2, N1, N2 = range(10)


def contract_rows(a, b):
    return lax.dot_general(a, b, (((0,), (0,)), ((), ())), preferred_element_type=F32)


def kernel(
    acts_h, mod_h, win_h, wout_h, zw_h, cot_h,
    block_o, grad_o, A16,
    acts, mod, win, wout, zw, cot, in_sem,
    parts, cols, xf, normed, pre, dgelu, hidden, T, stat,
    sC, rC1, mC32, mC16, rC2,
    sB, rB1, mB32, mB16, rB2,
    sN, rN1, mN32, mN16, rN2,
    GG, GO, a2d, rows32, up32,
    carr_s, carr_r, co_s, co_r,
    st_s1, st_r1, st_s2, st_r2,
    cot1_r, zf, F16, zr1, H32, H16, zr2,
    ss, rs, st_ss, st_rs, g_ss, g_rs, c_ss, c_rs, z2_ss, z2_rs, z3_ss, z3_rs, z4_ss, z4_rs,
):
    g = lax.axis_index("grp")
    f = lax.axis_index("fsdp")
    d = lax.axis_index("dp")
    y, x = f // 4, f % 4
    z, c = d // 2, d % 2
    pos = g * 4 + z
    control = g == 0
    base = g == 1

    def at_xy(py, px):
        return (g, py * 4 + px, d)

    def at_z(q):
        return (q // 4, f, (q % 4) * 2 + c)

    sibling = (g, f, z * 2 + (1 - c))
    partner = (1 - g, f, d)

    loads = [
        pltpu.make_async_copy(src, dst, in_sem.at[i])
        for i, (src, dst) in enumerate(
            ((mod_h, mod), (cot_h.at[0], cot), (zw_h, zw), (acts_h.at[0], acts), (win_h.at[0], win), (wout_h.at[0], wout))
        )
    ]
    l_mod, l_cot, l_zw, l_acts, l_win, l_wout = loads
    l_mod.start()
    l_cot.start()

    @pl.when(base)
    def _():
        l_zw.start()

    l_acts.start()
    l_win.start()

    barrier = pltpu.get_barrier_semaphore()
    for k in (1, 2, 3):
        pl.semaphore_signal(barrier, inc=1, device_id=at_xy(y, (x + k) % 4), device_id_type=MESH)
        pl.semaphore_signal(barrier, inc=1, device_id=at_xy((y + k) % 4, x), device_id_type=MESH)
    for k in range(1, 8):
        pl.semaphore_signal(barrier, inc=1, device_id=at_z((pos + k) % 8), device_id_type=MESH)
    pl.semaphore_signal(barrier, inc=1, device_id=sibling, device_id_type=MESH)

    def remote(src, dst, send, recv, where):
        return pltpu.make_async_remote_copy(
            src_ref=src, dst_ref=dst, send_sem=send, recv_sem=recv, device_id=where, device_id_type=MESH
        )

    HK = [(h, k) for k in (1, 3, 2) for h in (0, 1)]

    def peer_x(k):
        return at_xy(y, (x + k) % 4)

    def peer_y(k):
        return at_xy((y + k) % 4, x)

    def rs1(n, s, r1):
        out = []
        for h, k in HK:
            to = (x + k) % 4 if h == 0 else (y + k) % 4
            where = peer_x(k) if h == 0 else peer_y(k)
            out.append(remote(s.at[h, to], r1.at[h, k - 1], ss.at[n, h, k - 1], rs.at[n, h, k - 1], where))
        return out

    def rs2(n, m16, r2):
        out = []
        for h, k in HK:
            to = (y + k) % 4 if h == 0 else (x + k) % 4
            where = peer_y(k) if h == 0 else peer_x(k)
            out.append(remote(m16.at[h, to], r2.at[h, k - 1], ss.at[n, h, k - 1], rs.at[n, h, k - 1], where))
        return out

    def ag1(n, G):
        out = []
        for h, k in HK:
            blk = G.at[0, x, y] if h == 0 else G.at[1, y, x]
            where = peer_y(k) if h == 0 else peer_x(k)
            out.append(remote(blk, blk, ss.at[n, h, k - 1], rs.at[n, h, k - 1], where))
        return out

    def ag2(n, G):
        out = []
        for h, k in HK:
            blk = G.at[0, x] if h == 0 else G.at[1, y]
            where = peer_x(k) if h == 0 else peer_y(k)
            out.append(remote(blk, blk, ss.at[n, h, k - 1], rs.at[n, h, k - 1], where))
        return out

    def ag_block(n, G, h, j):
        if h == 0:
            blk = G.at[0, x, (y + 4 - j) % 4]
            return [remote(blk, blk, ss.at[n, 0, k - 1], rs.at[n, 0, k - 1], peer_x(k)) for k in (1, 3, 2)]
        blk = G.at[1, y, (x + 4 - j) % 4]
        return [remote(blk, blk, ss.at[n, 1, k - 1], rs.at[n, 1, k - 1], peer_y(k)) for k in (1, 3, 2)]

    def ag_start(n, G):
        start(ag1(n, G) + ag_block(n + 1, G, 0, 0) + ag_block(n + 1, G, 1, 0))

    def ag_forward(n, G):
        for (h, j), cp in zip(HK, ag1(n, G)):
            cp.wait_recv()
            start(ag_block(n + 1, G, h, j))

    def start(copies):
        for cp in copies:
            cp.start()

    def arrived(copies):
        for cp in copies:
            cp.wait_recv()

    def sent(copies):
        for cp in copies:
            cp.wait_send()

    def extract(s):
        def body(i, _):
            blk = T[pl.ds(pl.multiple_of(i * B, 8), B), :]
            s[0, i % 4, i // 4] = blk[:, :L].astype(BF16)
            s[1, i // 4, i % 4] = blk[:, L:].astype(BF16)
            return 0

        lax.fori_loop(0, 16, body, 0)

    def rs_mid(s, r1, m32, m16):
        def body(q, _):
            for h in (0, 1):
                own = x if h == 0 else y
                total = s[h, own, q].astype(F32)
                for k in range(3):
                    total = total + r1[h, k, q].astype(F32)
                m32[h, q] = total
                m16[h, q] = total.astype(BF16)
            return 0

        lax.fori_loop(0, 4, body, 0)

    def rs_last(m32, r2, out):
        for h in (0, 1):
            total = m32[h, y if h == 0 else x]
            for k in range(3):
                total = total + r2[h, k].astype(F32)
            out[:, h * L : (h + 1) * L] = total

    def flatten(G):
        def body(i, _):
            yy, xx = i // 2, 2 * (i % 2)
            rows = pl.ds(pl.multiple_of(i * 2 * B, 16), 2 * B)
            for h in (0, 1):
                p, q = (G[0, xx, yy], G[0, xx + 1, yy]) if h == 0 else (G[1, yy, xx], G[1, yy, xx + 1])
                both = jnp.concatenate([p.astype(F32), q.astype(F32)], axis=0)
                a2d[rows, h * L : (h + 1) * L] = both.astype(BF16)
            return 0

        lax.fori_loop(0, 8, body, 0)

    copies_c1, copies_c2 = rs1(C1, sC, rC1), rs2(C2, mC16, rC2)
    copies_b1, copies_b2 = rs1(B1, sB, rB1), rs2(B2, mB16, rB2)
    copies_n1, copies_n2 = rs1(N1, sN, rN1), rs2(N2, mN16, rN2)
    copies_g1, copies_g2 = ag1(G1, GG), ag2(G2, GG)
    copies_o1, copies_o2 = ag1(O1, GO), ag2(O2, GO)
    carr_copy = remote(carr_s, carr_r, g_ss.at[0], g_rs.at[0], partner)
    co_copy = remote(co_s, co_r, g_ss.at[1], g_rs.at[1], partner)
    cot_copy = remote(cot, cot1_r, g_ss.at[2], g_rs.at[2], partner)
    st1 = [remote(st_s1, st_r1.at[k - 1], st_ss.at[0, k - 1], st_rs.at[0, k - 1], peer_x(k)) for k in (1, 2, 3)]
    st2 = [remote(st_s2, st_r2.at[k - 1], st_ss.at[1, k - 1], st_rs.at[1, k - 1], peer_y(k)) for k in (1, 2, 3)]
    z1 = [remote(F16.at[e, 1 - c], zr1.at[e], c_ss.at[e], c_rs.at[e], sibling) for e in range(E)]
    z2 = [
        [
            remote(
                H16.at[e, (pos + k) % 8], zr2.at[e, z], z2_ss.at[e, k - 1], z2_rs.at[e, z], at_z((pos + k) % 8)
            )
            for k in (1, 7, 2, 6, 3, 5, 4)
        ]
        for e in range(E)
    ]

    def z3_copy(e, i, blk, q):
        return remote(blk, blk, z3_ss.at[e, i], z3_rs.at[e, i], at_z(q % 8))

    near = [[z3_copy(e, i, A16.at[e, c, pos], pos + by) for i, by in enumerate((1, 7, 2, 6, 3, 5, 4))] for e in range(E)]
    z4 = [
        [
            remote(
                A16.at[e, c, (pos + k) % 8], A16.at[e, c, (pos + k) % 8], z4_ss.at[e, k], z4_rs.at[e, k], sibling
            )
            for k in range(8)
        ]
        for e in range(E)
    ]

    def z2_arrival(e, zz):
        return remote(H16.at[e, 0], zr2.at[e, zz], z2_ss.at[e, 0], z2_rs.at[e, zz], sibling)

    l_cot.wait()

    @pl.when(base)
    def _():
        l_zw.wait()
        for c0, width in TILES:
            T[c0 : c0 + width, :] = contract_rows(zw[:, c0 : c0 + width], cot[...])
        extract(sC)

    @pl.when(base)
    def _():
        pl.semaphore_wait(barrier, 14)
        start(copies_c1)
        cot_copy.start()

    l_mod.wait()
    row = lax.broadcasted_iota(jnp.int32, (16, L), 0)
    for j in range(D // L):
        at = slice(j * L, (j + 1) * L)
        value = jnp.zeros((16, L), F32)
        for n, m in enumerate((1.0 + mod[1, :, at], mod[0, :, at], mod[2, :, at])):
            high = m.astype(BF16).astype(F32)
            middle = (m - high).astype(BF16).astype(F32)
            for k, part in enumerate((high, middle, (m - high) - middle)):
                value = jnp.where(row == 3 * n + k, part, value)
        parts[:, at] = value.astype(BF16)
    which = lax.broadcasted_iota(jnp.int32, (16, 3 * L), 0) // 3
    column = lax.broadcasted_iota(jnp.int32, (16, 3 * L), 1) // L
    select = jnp.where(which == column, 1.0, 0.0).astype(BF16)
    for c0, width in TILES:
        cols[c0 : c0 + width, :] = contract_rows(parts[:, c0 : c0 + width], select)

    def twice(v):
        return jnp.concatenate([v, v], axis=1)

    def fold(v):
        return jnp.sum(v.reshape(L // 8, 8, N), axis=0)

    l_acts.wait()
    l_wout.start()
    total = jnp.zeros((8, N), F32)
    for j in range(D // L):
        v = acts[j * L : (j + 1) * L, :].astype(F32)
        xf[j * L : (j + 1) * L, :] = v
        total = total + fold(v)
    mean = jnp.sum(total, axis=0, keepdims=True) * (1.0 / D)
    total = jnp.zeros((8, N), F32)
    for j in range(D // L):
        v = xf[j * L : (j + 1) * L, :] - mean
        total = total + fold(v * v)
    variance = jnp.sum(total, axis=0, keepdims=True) * (1.0 / D)
    rstd = lax.rsqrt(variance + EPSILON)
    stat[0:1, :] = mean
    stat[1:2, :] = rstd
    for j in range(D // L):
        at = slice(j * L, (j + 1) * L)
        v = (xf[at, :] - mean) * rstd
        normed[at, :] = (v * twice(cols[at, :L]) + twice(cols[at, L : 2 * L])).astype(BF16)

    l_win.wait()
    half = H // 2
    for i in range(2):
        pre[i * half : (i + 1) * half, :] = jnp.dot(
            win[i * half : (i + 1) * half, :], normed[...], preferred_element_type=F32
        )

    def gelu_body(j, _):
        at = pl.ds(pl.multiple_of(j * 32, 32), 32)
        v = pre[at, :]
        v2 = v * v
        t = jnp.tanh(GELU_C * (v + 0.044715 * (v2 * v)))
        cdf = 0.5 * (1.0 + t)
        hidden[at, :] = (v * cdf).astype(BF16)
        dgelu[at, :] = cdf + 0.5 * v * (1.0 - t * t) * (GELU_C * (1.0 + 3.0 * 0.044715 * v2))
        return 0

    lax.fori_loop(0, H // 32, gelu_body, 0)
    l_wout.wait()

    def produce(n, weights, s, r1, send):
        for yy, (c0, width) in enumerate(TILES):
            T[c0 : c0 + width, :] = contract_rows(weights[:, c0 : c0 + width], hidden[...])
            for xx in range(4):
                blk = T[(yy * 4 + xx) * B : (yy * 4 + xx + 1) * B, :]
                s[0, xx, yy] = blk[:, :L].astype(BF16)
                s[1, yy, xx] = blk[:, L:].astype(BF16)

            @pl.when(send)
            def _():
                for k in (1, 3, 2):
                    to = (x + k) % 4
                    remote(
                        s.at[0, to, yy], r1.at[0, k - 1, yy], ss.at[n, 0, k - 1], rs.at[n, 0, k - 1], peer_x(k)
                    ).start()

            @pl.when(jnp.logical_and(send, y != yy))
            def _():
                k = (yy + 4 - y) % 4
                remote(
                    s.at[1, yy], r1.at[1, k - 1], ss.at[n, 1, k - 1], rs.at[n, 1, k - 1], at_xy(yy, x)
                ).start()

    @pl.when(control)
    def _():
        pl.semaphore_wait(barrier, 14)

    produce(B1, wout, sB, rB1, control)

    own_rows = pl.ds(pl.multiple_of(f * B, 8), B)
    gate_rows = twice(cols[own_rows, 2 * L :])

    def set_gate_grad(up):
        gg = (gate_rows * up).astype(BF16)
        GG[0, x, y] = gg[:, :L]
        GG[1, y, x] = gg[:, L:]

    @pl.when(base)
    def _():
        arrived(copies_c1)
        rs_mid(sC, rC1, mC32, mC16)
        start(copies_c2)
        up = cot[...].astype(F32)
        up32[...] = up
        set_gate_grad(up)
        start(copies_g1)
        arrived(copies_c2)
        rs_last(mC32, rC2, rows32)
        carr_s[...] = rows32[...].astype(BF16)
        carr_copy.start()
        start(copies_b1)
        arrived(copies_g1)
        start(copies_g2)

    def branch_mid():
        arrived(copies_b1)
        rs_mid(sB, rB1, mB32, mB16)
        start(copies_b2)

    def branch_rows():
        arrived(copies_b2)
        rs_last(mB32, rB2, rows32)
        rows32[...] = xf[own_rows, :] + gate_rows * rows32[...]

    @pl.when(control)
    def _():
        branch_mid()
        branch_rows()
        out = rows32[...].astype(BF16)
        block_o[...] = out
        co_s[...] = out
        co_copy.start()
        GO[0, x, y] = out[:, :L]
        GO[1, y, x] = out[:, L:]
        ag_start(O1, GO)
        carr_copy.wait_recv()
        up = carr_r[...].astype(F32) + cot[...].astype(F32)
        up32[...] = up
        set_gate_grad(up)
        start(copies_g1)
        ag_forward(O1, GO)
        cot_copy.wait_recv()
        zf[19 * B :, :] = jnp.zeros((16 * E * OWN - 19 * B, L), F32)

        arrived(copies_o2)
        arrived(copies_g1)
        start(copies_g2)
        flatten(GO)
        for c0, width in TILES:
            term = lax.dot_general(
                cot1_r[...], a2d[c0 : c0 + width, :], (((1,), (1,)), ((), ())), preferred_element_type=F32
            )
            for t in range(width // L):
                r0 = (c0 // L + t) * B
                zf[r0 : r0 + B, :] = term[:, t * L : (t + 1) * L]

        for e in range(E):

            def flat_body(o, _):
                at = pl.ds(pl.multiple_of((e * 16 + o) * OWN, OWN), OWN)
                F16[e, o // 8, o % 8] = zf[at, :].astype(BF16)
                return 0

            lax.fori_loop(0, 16, flat_body, 0)
            z1[e].start()

    @pl.when(base)
    def _():
        co_copy.wait_recv()
        GO[0, x, y] = co_r[:, :L]
        GO[1, y, x] = co_r[:, L:]
        start(copies_o1)

    @pl.when(control)
    def _():
        for e in range(E):
            z1[e].wait_recv()

            def pair_body(q, _):
                at = pl.ds(pl.multiple_of((e * 16 + c * 8 + q) * OWN, OWN), OWN)
                total = zf[at, :] + zr1[e, q].astype(F32)
                H32[e, q] = total
                H16[e, q] = total.astype(BF16)
                return 0

            lax.fori_loop(0, 8, pair_body, 0)
            start(z2[e])

    arrived(copies_g2)
    flatten(GG)
    for i in range(2):
        hg = jnp.dot(wout[i * half : (i + 1) * half, :], a2d[...], preferred_element_type=F32)
        hidden[i * half : (i + 1) * half, :] = (hg * dgelu[i * half : (i + 1) * half, :]).astype(BF16)

    @pl.when(base)
    def _():
        arrived(copies_o1)
        start(copies_o2)

    produce(N1, win, sN, rN1, g >= 0)
    p1 = jnp.zeros((8, N), F32)
    p2 = jnp.zeros((8, N), F32)
    for j in range(D // L):
        at = slice(j * L, (j + 1) * L)
        v = T[at, :] * twice(cols[at, :L])
        p1 = p1 + fold(v)
        p2 = p2 + fold(v * ((xf[at, :] - stat[0:1, :]) * stat[1:2, :]))
    st_s1[0:8, :] = p1
    st_s1[8:16, :] = p2
    start(st1)

    @pl.when(base)
    def _():
        branch_mid()

    for e in range(E):

        @pl.when(control)
        def _():
            for k in (1, 2, 3):
                z2_arrival(e, (z + k) % 4).wait_recv()
            total = H32[e, pos]
            for k in (1, 2, 3):
                total = total + zr2[e, (z + k) % 4].astype(F32)
            A16[e, c, pos] = total.astype(BF16)

        @pl.when(base)
        def _():
            for k in range(4):
                z2_arrival(e, k).wait_recv()
            total = zr2[e, 0].astype(F32)
            for k in (1, 2, 3):
                total = total + zr2[e, k].astype(F32)
            A16[e, c, pos] = total.astype(BF16)

        start(near[e])
        z4[e][0].start()

    arrived(copies_n1)
    rs_mid(sN, rN1, mN32, mN16)
    start(copies_n2)
    arrived(st1)
    st_s2[...] = st_s1[...] + st_r1[0] + st_r1[1] + st_r1[2]
    start(st2)

    @pl.when(base)
    def _():
        branch_rows()
        arrived(copies_o2)
        flatten(GO)
        residual = jnp.dot(zw[...], a2d[...], preferred_element_type=F32)
        block_o[...] = (rows32[...] + residual).astype(BF16)

    for e in range(E):
        for cp, k in zip(near[e], (7, 1, 6, 2, 5, 3, 4)):
            cp.wait_recv()
            z4[e][k].start()

    arrived(copies_n2)
    arrived(st2)
    rs_last(mN32, rN2, rows32)
    both = st_s2[...] + st_r2[0] + st_r2[1] + st_r2[2]
    m1 = jnp.sum(both[0:8, :], axis=0, keepdims=True) * (1.0 / D)
    m2 = jnp.sum(both[8:16, :], axis=0, keepdims=True) * (1.0 / D)
    xhat = (xf[own_rows, :] - stat[0:1, :]) * stat[1:2, :]
    ghat = rows32[...] * twice(cols[own_rows, :L])
    grad_o[...] = up32[...] + stat[1:2, :] * (ghat - m1 - xhat * m2)

    for e in range(E):
        arrived(z4[e])

    sent(copies_b1 + copies_b2 + copies_g1 + copies_g2 + copies_o1 + copies_o2 + copies_n1 + copies_n2)
    sent(st1 + st2)
    for e in range(E):
        sent(near[e] + z4[e])

    @pl.when(base)
    def _():
        sent(copies_c1 + copies_c2 + [carr_copy, cot_copy])

    @pl.when(control)
    def _():
        sent(z1 + [co_copy])
        for e in range(E):
            sent(z2[e])


def finish(block, grad, flat, block_o, grad_o, zero_o, flat_v, zf, rows, block_v, grad_v, sem):
    def move(src, dst, i):
        cp = pltpu.make_async_copy(src, dst, sem.at[i])
        cp.start()
        return cp

    ins = [move(flat, flat_v, 0), move(grad, grad_v, 1), move(block, block_v, 2)]
    ins[1].wait()
    outs = [move(grad_v, grad_o.at[0], 3)]
    ins[2].wait()
    outs.append(move(block_v, block_o.at[0], 4))
    ins[0].wait()
    for i, (o0, o1, t0, t1) in enumerate(((0, 16, 0, 10), (16, 32, 10, 19))):
        for o in range(o0, o1):
            zf[o * OWN : (o + 1) * OWN, :] = flat_v[o // 16, (o // 8) % 2, o % 8].astype(F32)
        for t in range(t0, t1):
            rows[:, t * L : (t + 1) * L] = zf[t * B : (t + 1) * B, :]
        part = pl.ds(t0 * L, (t1 - t0) * L)
        outs.append(move(rows.at[:, part], zero_o.at[:, part], 5 + i))
    for cp in outs:
        cp.wait()


def local(acts, modulation, w_in, w_out, zero_weight, cotangent):
    vm = pltpu.VMEM
    dma = pltpu.SemaphoreType.DMA

    def rs_bufs():
        return [vm((2, 4, 4, B, L), BF16), vm((2, 3, 4, B, L), BF16), vm((2, 4, B, L), F32), vm((2, 4, B, L), BF16), vm((2, 3, B, L), BF16)]

    scratch = [
        vm((D, N), BF16), vm((3, 1, D), F32), vm((H, D), BF16), vm((H, D), BF16), vm((B, D), BF16), vm((B, N), BF16), dma((6,)),
        vm((16, D), BF16), vm((D, 3 * L), F32), vm((D, N), F32), vm((D, N), BF16), vm((H, N), F32), vm((H, N), F32), vm((H, N), BF16), vm((D, N), F32), vm((8, N), F32),
        *rs_bufs(), *rs_bufs(), *rs_bufs(),
        vm((2, 4, 4, B, L), BF16), vm((2, 4, 4, B, L), BF16), vm((D, N), BF16), vm((B, N), F32), vm((B, N), F32),
        vm((B, N), BF16), vm((B, N), BF16), vm((B, N), BF16), vm((B, N), BF16),
        vm((16, N), F32), vm((3, 16, N), F32), vm((16, N), F32), vm((3, 16, N), F32),
        vm((B, N), BF16), vm((16 * E * OWN, L), F32), vm((E, 2, 8, OWN, L), BF16), vm((E, 8, OWN, L), BF16),
        vm((E, 8, OWN, L), F32), vm((E, 8, OWN, L), BF16), vm((E, 4, OWN, L), BF16),
        dma((10, 2, 3)), dma((10, 2, 3)), dma((2, 3)), dma((2, 3)), dma((3,)), dma((3,)), dma((E,)), dma((E,)),
        dma((E, 7)), dma((E, 4)), dma((E, 7)), dma((E, 7)), dma((E, 8)), dma((E, 8)),
    ]
    results = pl.pallas_call(
        kernel,
        out_shape=(
            jax.ShapeDtypeStruct((B, N), BF16),
            jax.ShapeDtypeStruct((B, N), F32),
            jax.ShapeDtypeStruct((E, 2, 8, OWN, L), BF16),
        ),
        in_specs=[pl.BlockSpec(memory_space=pl.ANY)] * 6,
        out_specs=[pl.BlockSpec(memory_space=pltpu.VMEM)] * 3,
        scratch_shapes=scratch,
        compiler_params=pltpu.CompilerParams(
            collective_id=0, has_side_effects=True, vmem_limit_bytes=60 * 2**20
        ),
    )(acts, jnp.transpose(modulation, (1, 0, 2)), w_in, w_out, zero_weight, cotangent)
    return pl.pallas_call(
        finish,
        out_shape=(
            jax.ShapeDtypeStruct((1, B, N), BF16),
            jax.ShapeDtypeStruct((1, B, N), F32),
            jax.ShapeDtypeStruct((B, D), F32),
        ),
        in_specs=[pl.BlockSpec(memory_space=pl.ANY)] * 3,
        out_specs=[pl.BlockSpec(memory_space=pl.ANY)] * 3,
        scratch_shapes=[vm((E, 2, 8, OWN, L), BF16), vm((16 * E * OWN, L), F32), vm((B, D), F32), vm((B, N), BF16), vm((B, N), F32), dma((7,))],
        compiler_params=pltpu.CompilerParams(vmem_limit_bytes=60 * 2**20),
    )(*results)


def solution(mesh):
    placed = (
        P("grp", None, "dp"),
        P("grp", None, None),
        P("grp", "fsdp", None),
        P("grp", "fsdp", None),
        P("fsdp", None),
        P("grp", "fsdp", "dp"),
    )
    return jax.shard_map(
        local,
        mesh=mesh,
        in_specs=placed,
        out_specs=(P("grp", "fsdp", "dp"), P("grp", "fsdp", "dp"), P("fsdp", None)),
        check_vma=False,
    )
```
